512 devices in a mesh: expert: 64 (over z_lo, y, core), tensor: 8 (over x, z_hi).
Axes of the slice: x: 4, y: 4, z: 16 (z_hi: 2, z_lo: 8; z = z_hi * 8 + z_lo), core: 2. Of those that a mesh axis runs over, the one named last changes fastest.
Arguments:
- tokens: bfloat16 [8192, 2048], P('expert', 'tensor'), may hold values from -6 to 6
- upstream: bfloat16 [8192, 2048], P('expert', 'tensor'), may hold values from -6 to 6
- probs: bfloat16 [8192, 6], P('expert'), may hold values from 0.049804688 to 1
- expert_ids: int32 [8192, 6], P('expert'), may hold values from 0 to 63, all different within a row; in each aligned block of 128 rows (0 to 127, 128 to 255, ...) at most 16 rows name the same one
- gate_weight: bfloat16 [64, 1408, 2048], P('expert', 'tensor'), may hold values from -0.125 to 0.125
- up_weight: bfloat16 [64, 1408, 2048], P('expert', 'tensor'), may hold values from -0.125 to 0.125
- down_weight: bfloat16 [64, 1408, 2048], P('expert', 'tensor'), may hold values from -0.15625 to 0.15625
Outputs:
- grad_tokens: bfloat16 [8192, 2048], P('expert', 'tensor')
- grad_probs: bfloat16 [8192, 6], P('expert')
- grad_gate: bfloat16 [64, 1408, 2048], P('expert', 'tensor')
- grad_up: bfloat16 [64, 1408, 2048], P('expert', 'tensor')
- grad_down: bfloat16 [64, 1408, 2048], P('expert', 'tensor')
The draws below stay inside these ranges and needn't reach their ends.
Inputs may be any that keep to these rules, and one draw needn't show every extreme that they name: `expert_ids`: each token names 6 different experts. Among the 128 tokens of one aligned block no expert is named more than 16 times, and in every draw some expert is named exactly 16 times in some block; every expert is named by some token.
All inputs are finite; a program needn't handle non-finite values.
Results may differ from the reference program's by a relative error of at most 0.018.
Values may be sent and summed in bfloat16 or wider, within the bound.
A program may use at most 64 MiB of HBM per device.

```python
import math
import jax
import jax.numpy as jnp
import numpy as np
from jax import lax

D = 2048
FF = 1408
TOP = 6
TOK_DEV = 128
EXPERTS = 64
TOKENS = 8192
CAP = 16
N_TENSOR = 8


def levels(own_key, extent, pieces, least, top_value):
    def one(dim, blocks):
        draws = jax.random.uniform(jax.random.fold_in(jax.random.fold_in(own_key, 6), dim), (blocks,), jnp.float32, least / len(pieces), top_value / len(pieces))
        return jnp.repeat(jnp.exp(draws), extent[dim] // blocks).reshape((-1,) + (1,) * (len(extent) - dim - 1))

    factor_of = one(*pieces[0])
    for cut in pieces[1:]:
        factor_of = factor_of * one(*cut)
    return factor_of


def deal_out(stream_key, own, number, rows, number_of, top, most, lean):
    ranking = jax.random.permutation(stream_key, number_of)
    crowded, usual = load_shares(number_of, rows * top, most, lean, True), load_shares(number_of, rows * top, most, lean, False)
    places = jnp.arange(number_of)

    def named(lengths, offset_by):
        used = int((lengths > 0).sum())
        fixed = max(1, used // 4)
        shifted = fixed + (places - fixed + offset_by * (used - fixed)) % max(1, number_of - fixed)
        return jnp.zeros((number_of,), jnp.int32).at[ranking[jnp.where(places < fixed, places, shifted)]].set(jnp.asarray(lengths, jnp.int32))

    lengths = jnp.where(number % 4 == 0, named(crowded, number // 4), named(usual, number - number // 4 - 1))
    mixed = jax.random.permutation(jax.random.fold_in(own, 3), number_of)
    source_of, sink = mixed[0:number_of // 2 * 2:2], mixed[1:number_of // 2 * 2:2]
    room = jnp.minimum(lengths[source_of] - 1, most - lengths[sink]) // 2
    room = jnp.where((source_of == ranking[0]) | (sink == ranking[0]) | (lengths[sink] == 0), 0, jnp.maximum(room, 0))
    shifted = jax.random.randint(jax.random.fold_in(own, 4), (number_of // 2,), 0, 1 << 20) % (room + 1)
    lengths = lengths.at[source_of].add(-shifted).at[sink].add(shifted)
    members = jnp.searchsorted(jnp.cumsum(lengths), jnp.arange(rows * top), side="right").astype(jnp.int32)
    listing = members.reshape(top, rows).T
    listing = listing[jax.random.permutation(jax.random.fold_in(own, 1), rows)]
    offset_by = jax.random.randint(jax.random.fold_in(own, 2), (rows, 1), 0, top)
    return jnp.take_along_axis(listing, (jnp.arange(top)[None, :] + offset_by) % top, axis=1)


def load_shares(number_of, total, reach, skew, full):
    portions = [(1 << 20) // math.isqrt(rank ** skew) + 1 for rank in range(1, number_of + 1)]
    largest = reach if full else min(reach, max(-(-total // number_of), total * portions[0] // sum(portions)))
    least = 1 if total - largest >= number_of - 1 else 0
    holding, surplus = [largest] + [least] * (number_of - 1), total - largest - least * (number_of - 1)
    while surplus > 0:
        movable = [i for i in range(1, number_of) if holding[i] < largest] or [i for i in range(1, number_of) if holding[i] < reach]
        whole, budget = sum([portions[i] for i in movable]), surplus
        for i in movable:
            extra = min(reach - holding[i], max(1, budget * portions[i] // whole), surplus)
            holding[i] = holding[i] + extra
            surplus = surplus - extra
    return np.array(holding)


def bell_draw(own_key, extent, width, most, pieces=(), held_as=jnp.bfloat16):
    drawn = jax.random.normal(own_key, extent, jnp.float32) * width
    if len(pieces) > 0:
        drawn = levels(own_key, extent, pieces, -0.22, 0.18) * drawn
    return jnp.clip(drawn, min=-most, max=most).astype(held_as)


def setup_inputs(seed: int = 0) -> dict:
    arg_keys = jax.random.split(jax.random.key(seed), 8)
    tokens = bell_draw(arg_keys[0], (TOKENS, D), 1.0, 6.0, ((0, 64), (1, 8)))
    upstream = bell_draw(arg_keys[1], (TOKENS, D), 1.0, 6.0, ((0, 64), (1, 8)))
    probs = jnp.clip(jnp.exp(math.log(1.0) - 2.9996462 * jax.random.uniform(arg_keys[2], (TOKENS, TOP), jnp.float32) ** levels(arg_keys[2], (TOKENS, TOP), ((0, 64),), -0.2, 0.2)), 0.049804688, 1.0).astype(jnp.bfloat16)
    expert_ids_keys = jax.random.split(jax.random.fold_in(arg_keys[3], 1), TOKENS // TOK_DEV)
    expert_ids_turns = jax.random.permutation(jax.random.fold_in(arg_keys[3], 3), TOKENS // TOK_DEV)
    expert_ids = jax.vmap(lambda own, number: deal_out(jax.random.fold_in(arg_keys[3], 2), own, number, TOK_DEV, EXPERTS, TOP, CAP, 1))(expert_ids_keys, expert_ids_turns).reshape((TOKENS, TOP))
    gate_weight = bell_draw(arg_keys[4], (EXPERTS, FF, D), D ** -0.5, 0.125, ((0, 64), (1, 8)))
    up_weight = bell_draw(arg_keys[5], (EXPERTS, FF, D), D ** -0.5, 0.125, ((0, 64), (1, 8)))
    down_weight = bell_draw(arg_keys[6], (EXPERTS, FF, D), FF ** -0.5, 0.15625, ((0, 64), (1, 8)))
    return {"tokens": tokens, "upstream": upstream, "probs": probs, "expert_ids": expert_ids, "gate_weight": gate_weight, "up_weight": up_weight, "down_weight": down_weight}


def reference(tokens, upstream, probs, expert_ids, gate_weight, up_weight, down_weight):
    blocks = TOKENS // TOK_DEV
    flat_ids = expert_ids.reshape(blocks, TOK_DEV * TOP)
    onehot = (flat_ids[:, :, None] == jnp.arange(EXPERTS, dtype=jnp.int32)[None, None, :]).astype(jnp.int32)
    before = jnp.cumsum(onehot, axis=1) - onehot
    slot = jnp.sum(before * onehot, axis=2)
    dest = flat_ids * (blocks * CAP) + jnp.arange(blocks, dtype=jnp.int32)[:, None] * CAP + slot
    dest = dest.reshape(-1).astype(jnp.int32)
    count = TOKENS * TOP
    owner = jnp.full((EXPERTS * blocks * CAP,), count, jnp.int32)
    owner = owner.at[dest].set(jnp.arange(count, dtype=jnp.int32)).reshape(EXPERTS, blocks * CAP)
    x_pad = jnp.concatenate([tokens, jnp.zeros((1, D), jnp.bfloat16)], axis=0)
    dy_pad = jnp.concatenate([upstream, jnp.zeros((1, D), jnp.bfloat16)], axis=0)
    p_pad = jnp.concatenate([probs.reshape(-1), jnp.zeros((1,), jnp.bfloat16)], axis=0)
    group = FF // N_TENSOR

    def one_expert(carry, inputs):
        grad_x, grad_p = carry
        rows, w_gate, w_up, w_down = inputs
        tok = (rows // TOP).astype(jnp.int32)
        xs = x_pad[tok]
        dys = dy_pad[tok]
        weight = p_pad[rows].astype(jnp.float32)
        a = jnp.dot(xs, w_gate.T, preferred_element_type=jnp.float32)
        u = jnp.dot(xs, w_up.T, preferred_element_type=jnp.float32)
        sig = jax.nn.sigmoid(a)
        act = a * sig
        hidden = (act * u).astype(jnp.bfloat16)
        g = jnp.dot(dys, w_down.T, preferred_element_type=jnp.float32)
        dp_rows = jnp.sum(hidden.astype(jnp.float32) * g, axis=1).astype(jnp.bfloat16)
        dh = weight[:, None] * g
        d_a = (dh * u * sig * (1.0 + a * (1.0 - sig))).astype(jnp.bfloat16)
        d_u = (dh * act).astype(jnp.bfloat16)
        total = jnp.zeros((rows.shape[0], D), jnp.float32)
        for piece in range(N_TENSOR):
            lo = piece * group
            term = jnp.dot(d_a[:, lo:lo + group], w_gate[lo:lo + group, :], preferred_element_type=jnp.float32)
            term = term + jnp.dot(d_u[:, lo:lo + group], w_up[lo:lo + group, :], preferred_element_type=jnp.float32)
            total = total + lax.optimization_barrier(term.astype(jnp.bfloat16)).astype(jnp.float32)
        dx_rows = total.astype(jnp.bfloat16)
        grad_gate = jnp.dot(d_a.T, xs, preferred_element_type=jnp.float32).astype(jnp.bfloat16)
        grad_up = jnp.dot(d_u.T, xs, preferred_element_type=jnp.float32).astype(jnp.bfloat16)
        scaled = (weight[:, None] * hidden.astype(jnp.float32)).astype(jnp.bfloat16)
        grad_down = jnp.dot(scaled.T, dys, preferred_element_type=jnp.float32).astype(jnp.bfloat16)
        grad_x = grad_x.at[tok].add(dx_rows.astype(jnp.float32))
        grad_p = grad_p.at[rows].add(dp_rows.astype(jnp.float32))
        return (grad_x, grad_p), (grad_gate, grad_up, grad_down)

    start = (jnp.zeros((TOKENS + 1, D), jnp.float32), jnp.zeros((count + 1,), jnp.float32))
    (grad_x, grad_p), (grad_gate, grad_up, grad_down) = lax.scan(one_expert, start, (owner, gate_weight, up_weight, down_weight))
    grad_tokens = grad_x[:TOKENS].astype(jnp.bfloat16)
    grad_probs = grad_p[:count].reshape(TOKENS, TOP).astype(jnp.bfloat16)
    return (grad_tokens, grad_probs, grad_gate, grad_up, grad_down)
```

```python
import jax
import jax.numpy as jnp
from jax import lax
from jax.experimental import pallas as pl
from jax.experimental.pallas import tpu as pltpu
from jax.sharding import Mesh
from jax.sharding import PartitionSpec as P

MESH = pl.DeviceIdType.MESH
F32 = jnp.float32
BF16 = jnp.bfloat16

ZL, NY, NC, NX, ZH = 8, 4, 2, 4, 2
NZ = ZL * ZH
YC = NY * NC
TOK = 128
TOP = 6
CAP = 16
FS = 256
HID = 176
META = 16
WIDE = 2 * FS
HALF = TOK // 2


def dot(a, b, ad=1, bd=0):
    return lax.dot_general(a, b, (((ad,), (bd,)), ((), ())), preferred_element_type=F32)


def arrived(ref, sem):
    pltpu.make_async_copy(ref, ref, sem).wait()


def kernel(
    tok, ups, prob, ids, wg, wu, wd,
    gtok, gprob, ggate, gup, gdown,
    held, ysend, wsend, rows_x, wrow, dau_t, ph_t, own, part_o, part_rl, buf_a, buf_b,
    fsend, frecv, gsend, zrecv, dpx,
    s_z, r_z, s_y, r_y, s_w, r_w, s_x, r_x, s_a, r_a, s_b, r_b, s_f, r_f, s_g, r_g, s_d, r_d,
):
    zl, zh = lax.axis_index("zl"), lax.axis_index("zh")
    x = lax.axis_index("x")
    me = lax.axis_index("y") * NC + lax.axis_index("c")
    z = zh * ZL + zl

    def at_z(place):
        return {"zl": lax.rem(place, ZL), "zh": lax.div(place, ZL)}

    def at_yc(place):
        return {"y": lax.div(place, NC), "c": lax.rem(place, NC)}

    right, left = {"x": lax.rem(x + 1, NX)}, {"x": lax.rem(x + 3, NX)}

    def send(src, dst, s_sem, r_sem, device):
        pltpu.make_async_remote_copy(
            src_ref=src, dst_ref=dst, send_sem=s_sem, recv_sem=r_sem,
            device_id=device, device_id_type=MESH,
        ).start()

    barrier = pltpu.get_barrier_semaphore()
    for d in range(1, NZ):
        pl.semaphore_signal(barrier, inc=1, device_id=at_z(lax.rem(z + d, NZ)), device_id_type=MESH)
    for d in range(1, YC):
        pl.semaphore_signal(barrier, inc=1, device_id=at_yc(lax.rem(me + d, YC)), device_id_type=MESH)
    for d in range(1, NX):
        pl.semaphore_signal(barrier, inc=1, device_id={"x": lax.rem(x + d, NX)}, device_id_type=MESH)

    row_id = lax.broadcasted_iota(jnp.int32, (TOK, TOK), 0)
    col_id = lax.broadcasted_iota(jnp.int32, (TOK, TOK), 1)
    eye = (row_id == col_id).astype(F32).astype(BF16)
    earlier = (row_id < col_id).astype(F32).astype(BF16)
    held[0, 0:TOK, 0:FS] = tok[...]
    held[0, 0:TOK, FS:WIDE] = ups[...]
    ids_t = dot(ids[...].astype(F32).astype(BF16), eye, 0, 0)
    prob_t = dot(prob[...], eye, 0, 0)
    expert = lax.broadcasted_iota(jnp.int32, (ZL * YC, TOK), 0).astype(F32)
    named = jnp.zeros((ZL * YC, TOK), F32)
    for k in range(TOP):
        named = named + jnp.where(ids_t[k : k + 1] == expert, 1.0, 0.0)
    before = dot(named.astype(BF16), earlier)
    line = lax.broadcasted_iota(jnp.int32, (META, TOK), 0)
    id_rows = jnp.zeros((META, TOK), F32)
    slot_rows = jnp.zeros((META, TOK), F32)
    prob_rows = jnp.zeros((META, TOK), F32)
    for k in range(TOP):
        slot = jnp.sum(jnp.where(ids_t[k : k + 1] == expert, before, 0.0), axis=0, keepdims=True)
        id_rows = jnp.where(line == k, ids_t[k : k + 1], id_rows)
        slot_rows = jnp.where(line == k, slot, slot_rows)
        prob_rows = jnp.where(line == k, prob_t[k : k + 1], prob_rows)
    held[0, TOK : TOK + META, 0:TOK] = id_rows.astype(BF16)
    held[0, TOK : TOK + META, TOK : 2 * TOK] = slot_rows.astype(BF16)
    held[0, TOK : TOK + META, 2 * TOK : 3 * TOK] = prob_rows.astype(BF16)
    held[0, TOK : TOK + META, 3 * TOK : 4 * TOK] = jnp.zeros((META, TOK), BF16)

    pl.semaphore_wait(barrier, NZ + YC + NX - 3)

    def source(p):
        odd = lax.rem(p, 2) == 1
        place = lax.rem(z + jnp.where(odd, NZ - lax.div(p + 1, 2), lax.div(p, 2)), NZ)
        return lax.rem(place, ZL), lax.div(place, ZL)

    def block_rows(block, count=TOK, extra=0):
        return pl.ds(pl.multiple_of(block * TOK + extra, CAP), count)

    row_f = row_id.astype(F32)

    def routing(p):
        meta = held[p, TOK : TOK + META, :].astype(F32)
        code = (meta[:, 0:TOK] - (zl * YC).astype(F32)) * CAP + meta[:, TOK : 2 * TOK]
        return code, meta[:, 2 * TOK : 3 * TOK]

    def spread(code, values):
        total = jnp.zeros((TOK, TOK), F32)
        for k in range(TOP):
            value = 1.0 if values is None else values[k : k + 1]
            total = total + jnp.where(row_f == code[k : k + 1], value, 0.0)
        return total

    def take_in(p):
        @pl.when(p > 0)
        def _():
            arrived(held.at[p], r_z.at[p])

        @pl.when(p == 0)
        def _():
            send(held.at[0], held.at[1], s_z, r_z.at[1], at_z(lax.rem(z + 1, NZ)))
            send(held.at[0], held.at[2], s_z, r_z.at[2], at_z(lax.rem(z + NZ - 1, NZ)))

        @pl.when((p > 0) & (p < NZ - 2))
        def _():
            step = jnp.where(lax.rem(p, 2) == 1, 1, NZ - 1)
            send(held.at[p], held.at[p + 2], s_z, r_z.at[p + 2], at_z(lax.rem(z + step, NZ)))

        block, half = source(p)
        code, weights = routing(p)
        pick = spread(code, None).astype(BF16)
        ysend[p] = dot(pick, held[p, 0:TOK, :]).astype(BF16)
        mine = block_rows(block, CAP, me * CAP)
        my_rows = pl.ds(pl.multiple_of(me * CAP, CAP), CAP)
        rows_x[0, half, mine, :] = ysend[p, my_rows, :]
        for d in range(1, YC):
            to = lax.rem(me + d, YC)
            theirs = pl.ds(pl.multiple_of(to * CAP, CAP), CAP)
            send(ysend.at[p, theirs, :], rows_x.at[0, half, mine, :], s_y, r_y.at[p], at_yc(to))

        @pl.when(p >= ZL)
        def _():
            q = p - ZL
            weight = jnp.sum(spread(code, weights), axis=1, keepdims=True)
            wsend[q] = jnp.broadcast_to(weight, (TOK, TOK)).astype(BF16)
            wrow[mine, :] = wsend[q, my_rows, :]
            for d in range(1, YC):
                to = lax.rem(me + d, YC)
                theirs = pl.ds(pl.multiple_of(to * CAP, CAP), CAP)
                send(wsend.at[q, theirs, :], wrow.at[mine, :], s_w, r_w.at[q], at_yc(to))

    def pass_on(p):
        block, half = source(p)
        rows = block_rows(block)
        arrived(ysend.at[p, pl.ds(0, TOK - CAP), :], r_y.at[p])

        @pl.when(p >= ZL)
        def _():
            arrived(wsend.at[p - ZL, pl.ds(0, TOK - CAP), :], r_w.at[p - ZL])

        send(rows_x.at[0, half, rows, :], rows_x.at[1, half, rows, :], s_x, r_x.at[p, 0], right)
        send(rows_x.at[0, half, rows, :], rows_x.at[2, half, rows, :], s_x, r_x.at[p, 1], left)

    def relay(p):
        block, half = source(p)
        rows = block_rows(block)
        low, high = block_rows(block, HALF), block_rows(block, HALF, HALF)
        arrived(rows_x.at[1, half, rows, :], r_x.at[p, 0])
        send(rows_x.at[1, half, low, :], rows_x.at[3, half, low, :], s_x, r_x.at[p, 2], right)
        arrived(rows_x.at[2, half, rows, :], r_x.at[p, 1])
        send(rows_x.at[2, half, high, :], rows_x.at[3, half, high, :], s_x, r_x.at[p, 3], left)

    def all_here(p):
        block, half = source(p)
        arrived(rows_x.at[3, half, block_rows(block, HALF), :], r_x.at[p, 2])
        arrived(rows_x.at[3, half, block_rows(block, HALF, HALF), :], r_x.at[p, 3])

    def features(slot, half):
        shift = (0, 3, 1, 2)[slot] if isinstance(slot, int) else jnp.where(
            slot == 0, 0, jnp.where(slot == 1, 3, slot - 1)
        )
        return pl.ds(pl.multiple_of((lax.rem(x + shift, NX) * ZH + half) * FS, FS), FS)

    def compute(p):
        q = p - ZL
        block, _ = source(p)
        rows = block_rows(block)
        a = jnp.zeros((TOK, HID), F32)
        u = jnp.zeros((TOK, HID), F32)
        g = jnp.zeros((TOK, HID), F32)
        for slot in range(NX):
            for half in range(ZH):
                f = features(slot, half)
                xs = rows_x[slot, half, rows, 0:FS]
                dys = rows_x[slot, half, rows, FS:WIDE]
                a = a + dot(xs, wg[0, :, f], 1, 1)
                u = u + dot(xs, wu[0, :, f], 1, 1)
                g = g + dot(dys, wd[0, :, f], 1, 1)
        weight = wrow[rows, :].astype(F32)[:, 0:1]
        sig = jax.nn.sigmoid(a)
        act = a * sig
        hidden = (act * u).astype(BF16).astype(F32)
        dp = jnp.sum(hidden * g, axis=1, keepdims=True)
        fsend[q, :, WIDE : WIDE + TOK] = jnp.broadcast_to(dp, (TOK, TOK)).astype(BF16)
        dh = weight * g
        d_a = dh * u * sig * (1.0 + a * (1.0 - sig))
        d_u = dh * act
        lanes = pl.ds(pl.multiple_of(block * TOK, TOK), TOK)
        dau_t[0:HID, lanes] = d_a.T.astype(BF16)
        dau_t[HID : 2 * HID, lanes] = d_u.T.astype(BF16)
        ph_t[:, lanes] = (weight * hidden).T.astype(BF16)
        d_a = d_a.astype(BF16)
        d_u = d_u.astype(BF16)
        for slot in (3, 2, 1, 0):
            for half in range(ZH):
                f = features(slot, half)
                to = slice(half * FS, half * FS + FS)
                term = dot(d_a, wg[0, :, f]) + dot(d_u, wu[0, :, f])
                if slot == 0:
                    own[q, :, to] = term
                elif slot == 3:
                    part_o[q, :, to] = term.astype(BF16)
                else:
                    part_rl[2 - slot, q, :, to] = term.astype(BF16)
            if slot == 3:
                send(part_o.at[q, pl.ds(0, HALF), :], buf_a.at[0, q], s_a, r_a.at[q, 0], right)
                send(part_o.at[q, pl.ds(HALF, HALF), :], buf_a.at[1, q], s_a, r_a.at[q, 1], left)

    def add_relay(p):
        q = p - ZL
        arrived(buf_a.at[0, q], r_a.at[q, 0])
        part_rl[0, q, 0:HALF, :] = (
            part_rl[0, q, 0:HALF, :].astype(F32) + buf_a[0, q].astype(F32)
        ).astype(BF16)
        send(part_rl.at[0, q], buf_b.at[0, q], s_b, r_b.at[q, 0], right)
        arrived(buf_a.at[1, q], r_a.at[q, 1])
        part_rl[1, q, HALF:TOK, :] = (
            part_rl[1, q, HALF:TOK, :].astype(F32) + buf_a[1, q].astype(F32)
        ).astype(BF16)
        send(part_rl.at[1, q], buf_b.at[1, q], s_b, r_b.at[q, 1], left)

    def send_back(p):
        q = p - ZL
        arrived(buf_b.at[0, q], r_b.at[q, 0])
        arrived(buf_b.at[1, q], r_b.at[q, 1])
        fsend[q, :, 0:WIDE] = (
            own[q] + buf_b[0, q].astype(F32) + buf_b[1, q].astype(F32)
        ).astype(BF16)
        my_rows = pl.ds(pl.multiple_of(me * CAP, CAP), CAP)
        frecv[q, my_rows, :] = fsend[q, my_rows, :]
        for d in range(1, YC):
            to = lax.rem(me + d, YC)
            theirs = pl.ds(pl.multiple_of(to * CAP, CAP), CAP)
            send(fsend.at[q, theirs, :], frecv.at[q, my_rows, :], s_f, r_f.at[q], at_yc(to))

    def combine(p):
        q = p - ZL
        block, _ = source(p)
        arrived(fsend.at[q, pl.ds(0, TOK - CAP), :], r_f.at[q])
        code, _ = routing(p)
        pick = spread(code, None).astype(BF16)
        total = dot(pick, frecv[q, :, 0:WIDE], 0, 0).astype(BF16)
        dp = frecv[q, :, WIDE : WIDE + TOK].astype(F32)
        dp_rows = jnp.zeros((META, TOK), F32)
        for k in range(TOP):
            one = jnp.sum(jnp.where(row_f == code[k : k + 1], dp, 0.0), axis=0, keepdims=True)
            dp_rows = jnp.where(line == k, one, dp_rows)
        for half in range(ZH):
            gsend[q, half, 0:TOK, :] = total[:, half * FS : half * FS + FS]
            gsend[q, half, TOK : TOK + META, 0:TOK] = dp_rows.astype(BF16)
            gsend[q, half, TOK : TOK + META, TOK : 2 * TOK] = jnp.zeros((META, TOK), BF16)

        @pl.when(q < ZL - 1)
        def _():
            for half in range(ZH):
                to = block + half * ZL
                send(gsend.at[q, half], zrecv.at[lax.rem(to + NZ - z, NZ)], s_g, r_g, at_z(to))

        @pl.when(q == ZL - 1)
        def _():
            zrecv[0] = gsend[ZL - 1, zh]
            send(gsend.at[ZL - 1, 1 - zh], zrecv.at[ZL], s_g, r_g, at_z(lax.rem(z + ZL, NZ)))

    def weight_grads(slot):
        for half in range(ZH):
            f = features(slot, half)
            both = dot(dau_t[...], rows_x[slot, half, :, 0:FS])
            ggate[0, :, f] = both[0:HID].astype(BF16)
            gup[0, :, f] = both[HID : 2 * HID].astype(BF16)
            gdown[0, :, f] = dot(ph_t[...], rows_x[slot, half, :, FS:WIDE]).astype(BF16)

    def step(i, carry):
        def when(lag, least, act):
            p = i - lag

            @pl.when((p >= least) & (p < NZ))
            def _():
                act(p)

        when(0, 0, take_in)
        when(1, 0, pass_on)
        when(2, 0, relay)
        when(6, ZL, combine)
        when(5, ZL, send_back)
        when(4, ZL, add_relay)
        when(3, 0, all_here)
        when(3, ZL, compute)

        @pl.when(i >= NZ + 2)
        def _():
            weight_grads(i - (NZ + 2))

        return carry

    lax.fori_loop(0, NZ + 6, step, 0)

    arrived(zrecv.at[pl.ds(1, NZ - 1)], r_g)
    total = jnp.zeros((TOK, FS), F32)
    dp = jnp.zeros((META, TOK), F32)
    for s in range(NZ):
        total = total + zrecv[s, 0:TOK, :].astype(F32)
        dp = dp + zrecv[s, TOK : TOK + META, 0:TOK].astype(F32)
    dpx[x] = dp
    for d in range(1, NX):
        send(dpx.at[x], dpx.at[x], s_d, r_d, {"x": lax.rem(x + d, NX)})
    gtok[...] = total.astype(BF16)
    arrived(dpx.at[pl.ds(0, NX - 1)], r_d)
    dp = (dpx[0] + dpx[1]) + (dpx[2] + dpx[3])
    gprob[...] = dot(eye, dp.astype(BF16), 1, 1)[:, 0:TOP].astype(BF16)

    arrived(held.at[pl.ds(0, NZ - 1)], s_z)
    arrived(ysend.at[:, pl.ds(0, TOK - CAP), :], s_y)
    arrived(wsend.at[:, pl.ds(0, TOK - CAP), :], s_w)
    arrived(rows_x.at[pl.ds(1, NX - 1)], s_x)
    arrived(part_o, s_a)
    arrived(part_rl, s_b)
    arrived(fsend.at[:, pl.ds(0, TOK - CAP), :], s_f)
    arrived(zrecv.at[pl.ds(1, NZ - 1)], s_g)
    arrived(dpx.at[pl.ds(0, NX - 1)], s_d)


def body(tokens, upstream, probs, expert_ids, gate_weight, up_weight, down_weight):
    vmem = pl.BlockSpec(memory_space=pltpu.VMEM)
    dma = pltpu.SemaphoreType.DMA
    width = NX * ZH * FS
    out = (
        jax.ShapeDtypeStruct((TOK, FS), BF16),
        jax.ShapeDtypeStruct((TOK, TOP), BF16),
    ) + (jax.ShapeDtypeStruct((1, HID, width), BF16),) * 3
    return pl.pallas_call(
        kernel,
        out_shape=out,
        in_specs=[vmem] * 7,
        out_specs=(vmem,) * 5,
        scratch_shapes=[
            pltpu.VMEM((NZ, TOK + META, WIDE), BF16),
            pltpu.VMEM((NZ, TOK, WIDE), BF16),
            pltpu.VMEM((ZL, TOK, TOK), BF16),
            pltpu.VMEM((NX, ZH, ZL * TOK, WIDE), BF16),
            pltpu.VMEM((ZL * TOK, TOK), BF16),
            pltpu.VMEM((2 * HID, ZL * TOK), BF16),
            pltpu.VMEM((HID, ZL * TOK), BF16),
            pltpu.VMEM((ZL, TOK, WIDE), F32),
            pltpu.VMEM((ZL, TOK, WIDE), BF16),
            pltpu.VMEM((2, ZL, TOK, WIDE), BF16),
            pltpu.VMEM((2, ZL, HALF, WIDE), BF16),
            pltpu.VMEM((2, ZL, TOK, WIDE), BF16),
            pltpu.VMEM((ZL, TOK, WIDE + TOK), BF16),
            pltpu.VMEM((ZL, TOK, WIDE + TOK), BF16),
            pltpu.VMEM((ZL, ZH, TOK + META, FS), BF16),
            pltpu.VMEM((NZ, TOK + META, FS), BF16),
            pltpu.VMEM((NX, META, TOK), F32),
            dma, dma((NZ,)),
            dma, dma((NZ,)),
            dma, dma((ZL,)),
            dma, dma((NZ, 4)),
            dma, dma((ZL, 2)),
            dma, dma((ZL, 2)),
            dma, dma((ZL,)),
            dma, dma,
            dma, dma,
        ],
        compiler_params=pltpu.CompilerParams(
            collective_id=0, has_side_effects=True, vmem_limit_bytes=56 * 1024 * 1024
        ),
        cost_estimate=pl.CostEstimate(
            flops=16 * ZL * TOK * HID * width, bytes_accessed=8 << 20, transcendentals=0
        ),
    )(tokens, upstream, probs, expert_ids, gate_weight, up_weight, down_weight)


def solution(mesh):
    parts = Mesh(mesh.devices.reshape(ZL, NY, NC, NX, ZH), ("zl", "y", "c", "x", "zh"))
    expert, tensor = ("zl", "y", "c"), ("x", "zh")
    placed = (
        P(expert, tensor),
        P(expert, tensor),
        P(expert, None),
        P(expert, None),
        P(expert, tensor, None),
        P(expert, tensor, None),
        P(expert, tensor, None),
    )
    return jax.shard_map(
        body,
        mesh=parts,
        in_specs=placed,
        out_specs=(
            P(expert, tensor),
            P(expert, None),
            P(expert, tensor, None),
            P(expert, tensor, None),
            P(expert, tensor, None),
        ),
        check_vma=False,
    )
```

```python
import jax
import jax.numpy as jnp
from jax import lax
from jax.experimental import pallas as pl
from jax.experimental.pallas import tpu as pltpu
from jax.sharding import Mesh
from jax.sharding import PartitionSpec as P

MESH = pl.DeviceIdType.MESH
F32 = jnp.float32
BF16 = jnp.bfloat16

ZL, NY, NC, NX, ZH = 8, 4, 2, 4, 2
NZ = ZL * ZH
YC = NY * NC
TOK = 128
TOP = 6
CAP = 16
FS = 256
HID = 176
META = 16
WIDE = 2 * FS
HALF = TOK // 2
SUMS = 9


def dot(a, b, ad=1, bd=0):
    return lax.dot_general(a, b, (((ad,), (bd,)), ((), ())), preferred_element_type=F32)


def arrived(ref, sem):
    pltpu.make_async_copy(ref, ref, sem).wait()


def kernel(
    tok, ups, prob, ids, wg_far, wu_far, wd_far,
    gtok, gprob, ggate_far, gup_far, gdown_far,
    wg, wu, wd, ggate, gup, gdown, s_in, s_out,
    held, ysend, wsend, rows_x, wrow, dau_t, ph_t, own, part_o, part_rl, buf_a, buf_b,
    fsend, frecv, gsend, zrecv, chain, dpx,
    s_z, r_z, s_y, r_y, s_w, r_w, s_x, r_x, s_a, r_a, s_b, r_b, s_f, r_f, s_c, r_c, s_g, r_g, s_d, r_d,
):
    zl, zh = lax.axis_index("zl"), lax.axis_index("zh")
    x = lax.axis_index("x")
    me = lax.axis_index("y") * NC + lax.axis_index("c")
    z = zh * ZL + zl

    def at_z(place):
        return {"zl": lax.rem(place, ZL), "zh": lax.div(place, ZL)}

    def at_yc(place):
        return {"y": lax.div(place, NC), "c": lax.rem(place, NC)}

    right, left = {"x": lax.rem(x + 1, NX)}, {"x": lax.rem(x + 3, NX)}

    def send(src, dst, s_sem, r_sem, device):
        pltpu.make_async_remote_copy(
            src_ref=src, dst_ref=dst, send_sem=s_sem, recv_sem=r_sem,
            device_id=device, device_id_type=MESH,
        ).start()

    loads = [
        pltpu.make_async_copy(far.at[0], near, s_in.at[n])
        for n, (far, near) in enumerate(((wg_far, wg), (wu_far, wu), (wd_far, wd)))
    ]
    stores = [
        pltpu.make_async_copy(near, far.at[0], s_out.at[n])
        for n, (near, far) in enumerate(((ggate, ggate_far), (gup, gup_far), (gdown, gdown_far)))
    ]
    for load in loads:
        load.start()

    barrier = pltpu.get_barrier_semaphore()
    for d in range(1, NZ):
        pl.semaphore_signal(barrier, inc=1, device_id=at_z(lax.rem(z + d, NZ)), device_id_type=MESH)
    for d in range(1, YC):
        pl.semaphore_signal(barrier, inc=1, device_id=at_yc(lax.rem(me + d, YC)), device_id_type=MESH)
    for d in range(1, NX):
        pl.semaphore_signal(barrier, inc=1, device_id={"x": lax.rem(x + d, NX)}, device_id_type=MESH)

    row_id = lax.broadcasted_iota(jnp.int32, (TOK, TOK), 0)
    col_id = lax.broadcasted_iota(jnp.int32, (TOK, TOK), 1)
    earlier = (row_id < col_id).astype(F32).astype(BF16)
    held[0, 0:TOK, 0:FS] = tok[...]
    held[0, 0:TOK, FS:WIDE] = ups[...]
    ids_t = ids[...].astype(F32)
    prob_t = prob[...].astype(F32)
    expert = lax.broadcasted_iota(jnp.int32, (ZL * YC, TOK), 0).astype(F32)
    named = jnp.zeros((ZL * YC, TOK), F32)
    for k in range(TOP):
        named = named + jnp.where(ids_t[k : k + 1] == expert, 1.0, 0.0)
    before = dot(named.astype(BF16), earlier)
    line = lax.broadcasted_iota(jnp.int32, (META, TOK), 0)
    id_rows = jnp.zeros((META, TOK), F32)
    slot_rows = jnp.zeros((META, TOK), F32)
    prob_rows = jnp.zeros((META, TOK), F32)
    for k in range(TOP):
        slot = jnp.sum(jnp.where(ids_t[k : k + 1] == expert, before, 0.0), axis=0, keepdims=True)
        id_rows = jnp.where(line == k, ids_t[k : k + 1], id_rows)
        slot_rows = jnp.where(line == k, slot, slot_rows)
        prob_rows = jnp.where(line == k, prob_t[k : k + 1], prob_rows)
    held[0, TOK : TOK + META, 0:TOK] = id_rows.astype(BF16)
    held[0, TOK : TOK + META, TOK : 2 * TOK] = slot_rows.astype(BF16)
    held[0, TOK : TOK + META, 2 * TOK : 3 * TOK] = prob_rows.astype(BF16)
    held[0, TOK : TOK + META, 3 * TOK : 4 * TOK] = jnp.zeros((META, TOK), BF16)

    pl.semaphore_wait(barrier, NZ + YC + NX - 3)

    def source(p):
        odd = lax.rem(p, 2) == 1
        place = lax.rem(z + jnp.where(odd, NZ - lax.div(p + 1, 2), lax.div(p, 2)), NZ)
        return lax.rem(place, ZL), lax.div(place, ZL)

    def block_rows(block, count=TOK, extra=0):
        return pl.ds(pl.multiple_of(block * TOK + extra, CAP), count)

    row_f = row_id.astype(F32)

    def routing(p):
        meta = held[p, TOK : TOK + META, :].astype(F32)
        code = (meta[:, 0:TOK] - (zl * YC).astype(F32)) * CAP + meta[:, TOK : 2 * TOK]
        return code, meta[:, 2 * TOK : 3 * TOK]

    def spread(code, values):
        total = jnp.zeros((TOK, TOK), F32)
        for k in range(TOP):
            value = 1.0 if values is None else values[k : k + 1]
            total = total + jnp.where(row_f == code[k : k + 1], value, 0.0)
        return total

    def take_in(p):
        @pl.when(p > 0)
        def _():
            arrived(held.at[p], r_z.at[p])

        @pl.when(p == 0)
        def _():
            send(held.at[0], held.at[1], s_z, r_z.at[1], at_z(lax.rem(z + 1, NZ)))
            send(held.at[0], held.at[2], s_z, r_z.at[2], at_z(lax.rem(z + NZ - 1, NZ)))

        @pl.when((p > 0) & (p < NZ - 2))
        def _():
            step = jnp.where(lax.rem(p, 2) == 1, 1, NZ - 1)
            send(held.at[p], held.at[p + 2], s_z, r_z.at[p + 2], at_z(lax.rem(z + step, NZ)))

        block, half = source(p)
        code, weights = routing(p)
        pick = spread(code, None).astype(BF16)
        ysend[p] = dot(pick, held[p, 0:TOK, :]).astype(BF16)
        mine = block_rows(block, CAP, me * CAP)
        my_rows = pl.ds(pl.multiple_of(me * CAP, CAP), CAP)
        rows_x[0, half, mine, :] = ysend[p, my_rows, :]
        for d in range(1, YC):
            to = lax.rem(me + d, YC)
            theirs = pl.ds(pl.multiple_of(to * CAP, CAP), CAP)
            send(ysend.at[p, theirs, :], rows_x.at[0, half, mine, :], s_y, r_y.at[p], at_yc(to))

        @pl.when(p >= ZL)
        def _():
            q = p - ZL
            weight = jnp.sum(spread(code, weights), axis=1, keepdims=True)
            wsend[q] = jnp.broadcast_to(weight, (TOK, TOK)).astype(BF16)
            wrow[mine, :] = wsend[q, my_rows, :]
            for d in range(1, YC):
                to = lax.rem(me + d, YC)
                theirs = pl.ds(pl.multiple_of(to * CAP, CAP), CAP)
                send(wsend.at[q, theirs, :], wrow.at[mine, :], s_w, r_w.at[q], at_yc(to))

    def pass_on(p):
        block, half = source(p)
        rows = block_rows(block)
        arrived(ysend.at[p, pl.ds(0, TOK - CAP), :], r_y.at[p])

        @pl.when(p >= ZL)
        def _():
            arrived(wsend.at[p - ZL, pl.ds(0, TOK - CAP), :], r_w.at[p - ZL])

        send(rows_x.at[0, half, rows, :], rows_x.at[1, half, rows, :], s_x, r_x.at[p, 0], right)
        send(rows_x.at[0, half, rows, :], rows_x.at[2, half, rows, :], s_x, r_x.at[p, 1], left)

    def relay(p):
        block, half = source(p)
        rows = block_rows(block)
        low, high = block_rows(block, HALF), block_rows(block, HALF, HALF)
        arrived(rows_x.at[1, half, rows, :], r_x.at[p, 0])
        send(rows_x.at[1, half, low, :], rows_x.at[3, half, low, :], s_x, r_x.at[p, 2], right)
        arrived(rows_x.at[2, half, rows, :], r_x.at[p, 1])
        send(rows_x.at[2, half, high, :], rows_x.at[3, half, high, :], s_x, r_x.at[p, 3], left)

    def all_here(p):
        block, half = source(p)
        arrived(rows_x.at[3, half, block_rows(block, HALF), :], r_x.at[p, 2])
        arrived(rows_x.at[3, half, block_rows(block, HALF, HALF), :], r_x.at[p, 3])

    def features(slot, half):
        shift = (0, 3, 1, 2)[slot] if isinstance(slot, int) else jnp.where(
            slot == 0, 0, jnp.where(slot == 1, 3, slot - 1)
        )
        return pl.ds(pl.multiple_of((lax.rem(x + shift, NX) * ZH + half) * FS, FS), FS)

    def compute(p):
        q = p - ZL
        block, _ = source(p)
        rows = block_rows(block)
        a = jnp.zeros((TOK, HID), F32)
        u = jnp.zeros((TOK, HID), F32)
        g = jnp.zeros((TOK, HID), F32)
        for slot in range(NX):
            for half in range(ZH):
                f = features(slot, half)
                xs = rows_x[slot, half, rows, 0:FS]
                dys = rows_x[slot, half, rows, FS:WIDE]
                a = a + dot(xs, wg[:, f], 1, 1)
                u = u + dot(xs, wu[:, f], 1, 1)
                g = g + dot(dys, wd[:, f], 1, 1)
        weight = wrow[rows, :].astype(F32)[:, 0:1]
        sig = jax.nn.sigmoid(a)
        act = a * sig
        hidden = (act * u).astype(BF16).astype(F32)
        dp = jnp.sum(hidden * g, axis=1, keepdims=True)
        fsend[q, :, WIDE : WIDE + TOK] = jnp.broadcast_to(dp, (TOK, TOK)).astype(BF16)
        dh = weight * g
        d_a = dh * u * sig * (1.0 + a * (1.0 - sig))
        d_u = dh * act
        lanes = pl.ds(pl.multiple_of(block * TOK, TOK), TOK)
        dau_t[0:HID, lanes] = d_a.T.astype(BF16)
        dau_t[HID : 2 * HID, lanes] = d_u.T.astype(BF16)
        ph_t[:, lanes] = (weight * hidden).T.astype(BF16)
        d_a = d_a.astype(BF16)
        d_u = d_u.astype(BF16)
        for slot in (3, 2, 1, 0):
            for half in range(ZH):
                f = features(slot, half)
                to = slice(half * FS, half * FS + FS)
                term = dot(d_a, wg[:, f]) + dot(d_u, wu[:, f])
                if slot == 0:
                    own[q, :, to] = term
                elif slot == 3:
                    part_o[q, :, to] = term.astype(BF16)
                else:
                    part_rl[2 - slot, q, :, to] = term.astype(BF16)
            if slot == 3:
                send(part_o.at[q, pl.ds(0, HALF), :], buf_a.at[0, q], s_a, r_a.at[q, 0], right)
                send(part_o.at[q, pl.ds(HALF, HALF), :], buf_a.at[1, q], s_a, r_a.at[q, 1], left)

    def add_relay(p):
        q = p - ZL
        arrived(buf_a.at[0, q], r_a.at[q, 0])
        part_rl[0, q, 0:HALF, :] = (
            part_rl[0, q, 0:HALF, :].astype(F32) + buf_a[0, q].astype(F32)
        ).astype(BF16)
        send(part_rl.at[0, q], buf_b.at[0, q], s_b, r_b.at[q, 0], right)
        arrived(buf_a.at[1, q], r_a.at[q, 1])
        part_rl[1, q, HALF:TOK, :] = (
            part_rl[1, q, HALF:TOK, :].astype(F32) + buf_a[1, q].astype(F32)
        ).astype(BF16)
        send(part_rl.at[1, q], buf_b.at[1, q], s_b, r_b.at[q, 1], left)

    def send_back(p):
        q = p - ZL
        arrived(buf_b.at[0, q], r_b.at[q, 0])
        arrived(buf_b.at[1, q], r_b.at[q, 1])
        fsend[q, :, 0:WIDE] = (
            own[q] + buf_b[0, q].astype(F32) + buf_b[1, q].astype(F32)
        ).astype(BF16)
        my_rows = pl.ds(pl.multiple_of(me * CAP, CAP), CAP)
        frecv[q, my_rows, :] = fsend[q, my_rows, :]
        for d in range(1, YC):
            to = lax.rem(me + d, YC)
            theirs = pl.ds(pl.multiple_of(to * CAP, CAP), CAP)
            send(fsend.at[q, theirs, :], frecv.at[q, my_rows, :], s_f, r_f.at[q], at_yc(to))

    def combine(p, m):
        q = p - ZL
        block, far = source(p)
        near = 1 - far
        arrived(fsend.at[q, pl.ds(0, TOK - CAP), :], r_f.at[q])
        code, _ = routing(p)
        pick = spread(code, None).astype(BF16)
        gsend[q, :, 0:TOK, :] = jnp.stack(
            [dot(pick, frecv[q, :, h * FS : h * FS + FS], 0, 0) for h in range(ZH)]
        ).astype(BF16)
        dp = frecv[q, :, WIDE : WIDE + TOK].astype(F32)
        dp_rows = jnp.zeros((META, TOK), F32)
        for k in range(TOP):
            one = jnp.sum(jnp.where(row_f == code[k : k + 1], dp, 0.0), axis=0, keepdims=True)
            dp_rows = jnp.where(line == k, one, dp_rows)
        for half in range(ZH):
            gsend[q, half, TOK : TOK + META, 0:TOK] = dp_rows.astype(BF16)
            gsend[q, half, TOK : TOK + META, TOK : 2 * TOK] = jnp.zeros((META, TOK), BF16)

        def place(to):
            away = lax.rem(to + NZ - z, NZ)
            return jnp.where(away < 5, away, away - 7)

        @pl.when((m >= 2) & (m < 7))
        def _():
            arrived(chain.at[m], r_c.at[m])
            gsend[q, far] = (gsend[q, far].astype(F32) + chain[m].astype(F32)).astype(BF16)

        @pl.when(m == 7)
        def _():
            for n, half in ((8, far), (7, near)):
                arrived(chain.at[n], r_c.at[n])
                gsend[q, half] = (gsend[q, half].astype(F32) + chain[n].astype(F32)).astype(BF16)

        @pl.when(m < 7)
        def _():
            step = jnp.where(lax.rem(m, 2) == 0, 1, NZ - 1)
            send(gsend.at[q, far], chain.at[m + 2], s_c, r_c.at[m + 2], at_z(lax.rem(z + step, NZ)))

        @pl.when(m == 7)
        def _():
            to = block + far * ZL
            send(gsend.at[q, far], zrecv.at[place(to)], s_g, r_g, at_z(to))

        @pl.when(m > 0)
        def _():
            to = block + near * ZL
            send(gsend.at[q, near], zrecv.at[place(to)], s_g, r_g, at_z(to))

        @pl.when(m == 0)
        def _():
            zrecv[0] = gsend[q, near]

    def weight_grads(slot):
        for half in range(ZH):
            f = features(slot, half)
            both = dot(dau_t[...], rows_x[slot, half, :, 0:FS])
            ggate[:, f] = both[0:HID].astype(BF16)
            gup[:, f] = both[HID : 2 * HID].astype(BF16)
            gdown[:, f] = dot(ph_t[...], rows_x[slot, half, :, FS:WIDE]).astype(BF16)

    def turn(j):
        m = j - ZL
        late = jnp.where(lax.rem(j, 2) == 1, jnp.maximum(14 - m, ZL), jnp.minimum(NZ - m, NZ - 1))
        return jnp.where(j < ZL, j, late)

    def step(i, carry):
        def when(lag, least, act):
            j = i - lag

            @pl.when((j >= least) & (j < NZ))
            def _():
                act(turn(j), *((j - ZL,) if act is combine else ()))

        when(1, 0, pass_on)

        @pl.when((i > 0) & (i <= ZL))
        def _():
            take_in(2 * i - 1)

        @pl.when(i < ZL)
        def _():
            take_in(2 * i)

        when(2, 0, relay)
        when(6, ZL, combine)
        when(5, ZL, send_back)
        when(4, ZL, add_relay)
        when(3, 0, all_here)

        @pl.when(i == ZL)
        def _():
            for load in loads:
                load.wait()

        when(3, ZL, compute)

        @pl.when(i >= NZ + 2)
        def _():
            weight_grads(i - (NZ + 2))

        return carry

    lax.fori_loop(0, NZ + 6, step, 0)
    for store in stores:
        store.start()

    arrived(zrecv.at[pl.ds(1, SUMS - 1)], r_g)
    total = jnp.zeros((TOK, FS), F32)
    dp = jnp.zeros((META, TOK), F32)
    for s in range(SUMS):
        total = total + zrecv[s, 0:TOK, :].astype(F32)
        dp = dp + zrecv[s, TOK : TOK + META, 0:TOK].astype(F32)
    dpx[x] = dp
    for d in range(1, NX):
        send(dpx.at[x], dpx.at[x], s_d, r_d, {"x": lax.rem(x + d, NX)})
    gtok[...] = total.astype(BF16)
    arrived(dpx.at[pl.ds(0, NX - 1)], r_d)
    dp = (dpx[0] + dpx[1]) + (dpx[2] + dpx[3])
    gprob[...] = dp[0:TOP].astype(BF16)

    for store in stores:
        store.wait()

    arrived(held.at[pl.ds(0, NZ - 1)], s_z)
    arrived(ysend.at[:, pl.ds(0, TOK - CAP), :], s_y)
    arrived(wsend.at[:, pl.ds(0, TOK - CAP), :], s_w)
    arrived(rows_x.at[pl.ds(1, NX - 1)], s_x)
    arrived(part_o, s_a)
    arrived(part_rl, s_b)
    arrived(fsend.at[:, pl.ds(0, TOK - CAP), :], s_f)
    arrived(zrecv.at[pl.ds(1, SUMS - 1)], s_g)
    arrived(chain.at[pl.ds(2, 7)], s_c)
    arrived(dpx.at[pl.ds(0, NX - 1)], s_d)


def hand_over(*refs):
    sems = refs[-1]
    copies = [
        pltpu.make_async_copy(src, dst, sems.at[n])
        for n, (src, dst) in enumerate(zip(refs[:5], refs[5:10]))
    ]
    for copy in copies:
        copy.start()
    for copy in copies:
        copy.wait()


def body(tokens, upstream, probs, expert_ids, gate_weight, up_weight, down_weight):
    vmem = pl.BlockSpec(memory_space=pltpu.VMEM)
    anywhere = pl.BlockSpec(memory_space=pl.ANY)
    dma = pltpu.SemaphoreType.DMA
    width = NX * ZH * FS
    out = (
        jax.ShapeDtypeStruct((TOK, FS), BF16),
        jax.ShapeDtypeStruct((TOP, TOK), BF16),
    ) + (jax.ShapeDtypeStruct((1, HID, width), BF16),) * 3
    results = pl.pallas_call(
        kernel,
        out_shape=out,
        in_specs=[vmem] * 4 + [anywhere] * 3,
        out_specs=(vmem,) * 2 + (anywhere,) * 3,
        scratch_shapes=[pltpu.VMEM((HID, width), BF16)] * 6
        + [
            dma((3,)), dma((3,)),
            pltpu.VMEM((NZ, TOK + META, WIDE), BF16),
            pltpu.VMEM((NZ, TOK, WIDE), BF16),
            pltpu.VMEM((ZL, TOK, TOK), BF16),
            pltpu.VMEM((NX, ZH, ZL * TOK, WIDE), BF16),
            pltpu.VMEM((ZL * TOK, TOK), BF16),
            pltpu.VMEM((2 * HID, ZL * TOK), BF16),
            pltpu.VMEM((HID, ZL * TOK), BF16),
            pltpu.VMEM((ZL, TOK, WIDE), F32),
            pltpu.VMEM((ZL, TOK, WIDE), BF16),
            pltpu.VMEM((2, ZL, TOK, WIDE), BF16),
            pltpu.VMEM((2, ZL, HALF, WIDE), BF16),
            pltpu.VMEM((2, ZL, TOK, WIDE), BF16),
            pltpu.VMEM((ZL, TOK, WIDE + TOK), BF16),
            pltpu.VMEM((ZL, TOK, WIDE + TOK), BF16),
            pltpu.VMEM((ZL, ZH, TOK + META, FS), BF16),
            pltpu.VMEM((SUMS, TOK + META, FS), BF16),
            pltpu.VMEM((9, TOK + META, FS), BF16),
            pltpu.VMEM((NX, META, TOK), F32),
            dma, dma((NZ,)),
            dma, dma((NZ,)),
            dma, dma((ZL,)),
            dma, dma((NZ, 4)),
            dma, dma((ZL, 2)),
            dma, dma((ZL, 2)),
            dma, dma((ZL,)),
            dma, dma((9,)),
            dma, dma,
            dma, dma,
        ],
        compiler_params=pltpu.CompilerParams(
            collective_id=0, has_side_effects=True, vmem_limit_bytes=56 * 1024 * 1024
        ),
        cost_estimate=pl.CostEstimate(
            flops=16 * ZL * TOK * HID * width, bytes_accessed=8 << 20, transcendentals=0
        ),
    )(tokens, upstream, probs.T, expert_ids.T, gate_weight, up_weight, down_weight)
    tokens_out, probs_out, *weights_out = pl.pallas_call(
        hand_over,
        out_shape=out,
        in_specs=[vmem] * 5,
        out_specs=(anywhere,) * 5,
        scratch_shapes=[dma((5,))],
    )(*results)
    return (tokens_out, probs_out.T, *weights_out)


def solution(mesh):
    parts = Mesh(mesh.devices.reshape(ZL, NY, NC, NX, ZH), ("zl", "y", "c", "x", "zh"))
    expert, tensor = ("zl", "y", "c"), ("x", "zh")
    placed = (
        P(expert, tensor),
        P(expert, tensor),
        P(expert, None),
        P(expert, None),
        P(expert, tensor, None),
        P(expert, tensor, None),
        P(expert, tensor, None),
    )
    return jax.shard_map(
        body,
        mesh=parts,
        in_specs=placed,
        out_specs=(
            P(expert, tensor),
            P(expert, None),
            P(expert, tensor, None),
            P(expert, tensor, None),
            P(expert, tensor, None),
        ),
        check_vma=False,
    )
```

```python
import jax
import jax.numpy as jnp
from jax import lax
from jax.experimental import pallas as pl
from jax.experimental.pallas import tpu as pltpu
from jax.sharding import Mesh
from jax.sharding import PartitionSpec as P

MESH = pl.DeviceIdType.MESH
F32 = jnp.float32
BF16 = jnp.bfloat16

ZL, NY, NC, NX, ZH = 8, 4, 2, 4, 2
NZ = ZL * ZH
YC = NY * NC
TOK = 128
TOP = 6
CAP = 16
FS = 256
HID = 176
META = 16
WIDE = 2 * FS
HALF = TOK // 2
FAR_FIRST = (4, 3, 5, 2, 6, 1, 7)
SUMS = 9


def dot(a, b, ad=1, bd=0):
    return lax.dot_general(a, b, (((ad,), (bd,)), ((), ())), preferred_element_type=F32)


def arrived(ref, sem):
    pltpu.make_async_copy(ref, ref, sem).wait()


def kernel(
    tok, ups, prob, ids, wg_far, wu_far, wd_far,
    gtok, gprob, ggate_far, gup_far, gdown_far,
    wg, wu, wd, ggate, gup, gdown, s_in, s_out,
    held, ysend, wsend, rows_x, wrow, dau_t, ph_t, own, part_o, part_rl, buf_a, buf_b,
    fsend, frecv, gsend, zrecv, chain, dpx,
    s_z, r_z, s_y, r_y, s_w, r_w, s_x, r_x, s_a, r_a, s_b, r_b, s_f, r_f, s_c, r_c, s_g, r_g, s_d, r_d,
):
    zl, zh = lax.axis_index("zl"), lax.axis_index("zh")
    x = lax.axis_index("x")
    me = lax.axis_index("y") * NC + lax.axis_index("c")
    z = zh * ZL + zl

    def at_z(place):
        return {"zl": lax.rem(place, ZL), "zh": lax.div(place, ZL)}

    def at_yc(place):
        return {"y": lax.div(place, NC), "c": lax.rem(place, NC)}

    right, left = {"x": lax.rem(x + 1, NX)}, {"x": lax.rem(x + 3, NX)}

    def send(src, dst, s_sem, r_sem, device):
        pltpu.make_async_remote_copy(
            src_ref=src, dst_ref=dst, send_sem=s_sem, recv_sem=r_sem,
            device_id=device, device_id_type=MESH,
        ).start()

    loads = [
        pltpu.make_async_copy(far.at[0], near, s_in.at[n])
        for n, (far, near) in enumerate(((wg_far, wg), (wu_far, wu), (wd_far, wd)))
    ]
    stores = [
        pltpu.make_async_copy(near, far.at[0], s_out.at[n])
        for n, (near, far) in enumerate(((ggate, ggate_far), (gup, gup_far), (gdown, gdown_far)))
    ]
    for load in loads:
        load.start()

    barrier = pltpu.get_barrier_semaphore()
    for d in range(1, NZ):
        pl.semaphore_signal(barrier, inc=1, device_id=at_z(lax.rem(z + d, NZ)), device_id_type=MESH)
    for d in range(1, YC):
        pl.semaphore_signal(barrier, inc=1, device_id=at_yc(lax.rem(me + d, YC)), device_id_type=MESH)
    for d in range(1, NX):
        pl.semaphore_signal(barrier, inc=1, device_id={"x": lax.rem(x + d, NX)}, device_id_type=MESH)

    row_id = lax.broadcasted_iota(jnp.int32, (TOK, TOK), 0)
    col_id = lax.broadcasted_iota(jnp.int32, (TOK, TOK), 1)
    earlier = (row_id < col_id).astype(F32).astype(BF16)
    held[0, 0:TOK, 0:FS] = tok[...]
    held[0, 0:TOK, FS:WIDE] = ups[...]
    ids_t = ids[...].astype(F32)
    prob_t = prob[...].astype(F32)
    expert = lax.broadcasted_iota(jnp.int32, (ZL * YC, TOK), 0).astype(F32)
    named = jnp.zeros((ZL * YC, TOK), F32)
    for k in range(TOP):
        named = named + jnp.where(ids_t[k : k + 1] == expert, 1.0, 0.0)
    before = dot(named.astype(BF16), earlier)
    line = lax.broadcasted_iota(jnp.int32, (META, TOK), 0)
    id_rows = jnp.zeros((META, TOK), F32)
    slot_rows = jnp.zeros((META, TOK), F32)
    prob_rows = jnp.zeros((META, TOK), F32)
    for k in range(TOP):
        slot = jnp.sum(jnp.where(ids_t[k : k + 1] == expert, before, 0.0), axis=0, keepdims=True)
        id_rows = jnp.where(line == k, ids_t[k : k + 1], id_rows)
        slot_rows = jnp.where(line == k, slot, slot_rows)
        prob_rows = jnp.where(line == k, prob_t[k : k + 1], prob_rows)
    held[0, TOK : TOK + META, 0:TOK] = id_rows.astype(BF16)
    held[0, TOK : TOK + META, TOK : 2 * TOK] = slot_rows.astype(BF16)
    held[0, TOK : TOK + META, 2 * TOK : 3 * TOK] = prob_rows.astype(BF16)
    held[0, TOK : TOK + META, 3 * TOK : 4 * TOK] = jnp.zeros((META, TOK), BF16)

    pl.semaphore_wait(barrier, NZ + YC + NX - 3)

    def source(p):
        odd = lax.rem(p, 2) == 1
        place = lax.rem(z + jnp.where(odd, NZ - lax.div(p + 1, 2), lax.div(p, 2)), NZ)
        return lax.rem(place, ZL), lax.div(place, ZL)

    def block_rows(block, count=TOK, extra=0):
        return pl.ds(pl.multiple_of(block * TOK + extra, CAP), count)

    row_f = row_id.astype(F32)

    def routing(p):
        first = jnp.where(p < ZL, p, NZ - 1 - p)
        meta = held[first, TOK : TOK + META, :].astype(F32)
        code = (meta[:, 0:TOK] - (zl * YC).astype(F32)) * CAP + meta[:, TOK : 2 * TOK]
        return code, meta[:, 2 * TOK : 3 * TOK]

    def spread(code, values):
        total = jnp.zeros((TOK, TOK), F32)
        for k in range(TOP):
            value = 1.0 if values is None else values[k : k + 1]
            total = total + jnp.where(row_f == code[k : k + 1], value, 0.0)
        return total

    def take_in(p):
        @pl.when((p > 0) & (p < ZL))
        def _():
            arrived(held.at[p], r_z.at[p])

        @pl.when(p >= ZL)
        def _():
            arrived(held.at[p, pl.ds(0, TOK)], r_z.at[p])

        @pl.when(p == 0)
        def _():
            send(held.at[0], held.at[1], s_z.at[0], r_z.at[1], at_z(lax.rem(z + 1, NZ)))
            send(held.at[0], held.at[2], s_z.at[0], r_z.at[2], at_z(lax.rem(z + NZ - 1, NZ)))

        onward = at_z(lax.rem(z + jnp.where(lax.rem(p, 2) == 1, 1, NZ - 1), NZ))

        @pl.when((p > 0) & (p < ZL - 2))
        def _():
            send(held.at[p], held.at[p + 2], s_z.at[0], r_z.at[p + 2], onward)

        @pl.when((p >= ZL - 2) & (p < NZ - 2))
        def _():
            send(
                held.at[p, pl.ds(0, TOK)], held.at[p + 2, pl.ds(0, TOK)],
                s_z.at[1], r_z.at[p + 2], onward,
            )

    def pack(p):
        block, half = source(p)
        code, weights = routing(p)
        pick = spread(code, None).astype(BF16)
        ysend[p] = dot(pick, held[p, 0:TOK, :]).astype(BF16)
        mine = block_rows(block, CAP, me * CAP)
        my_rows = pl.ds(pl.multiple_of(me * CAP, CAP), CAP)
        rows_x[0, half, mine, :] = ysend[p, my_rows, :]
        for d in FAR_FIRST:
            to = lax.rem(me + d, YC)
            theirs = pl.ds(pl.multiple_of(to * CAP, CAP), CAP)
            send(ysend.at[p, theirs, :], rows_x.at[0, half, mine, :], s_y, r_y.at[p], at_yc(to))

        @pl.when(p >= ZL)
        def _():
            q = p - ZL
            weight = jnp.sum(spread(code, weights), axis=1, keepdims=True)
            wsend[q] = jnp.broadcast_to(weight, (TOK, TOK)).astype(BF16)
            wrow[mine, :] = wsend[q, my_rows, :]
            for d in FAR_FIRST:
                to = lax.rem(me + d, YC)
                theirs = pl.ds(pl.multiple_of(to * CAP, CAP), CAP)
                send(wsend.at[q, theirs, :], wrow.at[mine, :], s_w, r_w.at[q], at_yc(to))

    def pass_on(p):
        block, half = source(p)
        rows = block_rows(block)
        arrived(ysend.at[p, pl.ds(0, TOK - CAP), :], r_y.at[p])

        @pl.when(p >= ZL)
        def _():
            arrived(wsend.at[p - ZL, pl.ds(0, TOK - CAP), :], r_w.at[p - ZL])

        send(rows_x.at[0, half, rows, :], rows_x.at[1, half, rows, :], s_x, r_x.at[p, 0], right)
        send(rows_x.at[0, half, rows, :], rows_x.at[2, half, rows, :], s_x, r_x.at[p, 1], left)

    def relay(p):
        block, half = source(p)
        rows = block_rows(block)
        low, high = block_rows(block, HALF), block_rows(block, HALF, HALF)
        arrived(rows_x.at[1, half, rows, :], r_x.at[p, 0])
        send(rows_x.at[1, half, low, :], rows_x.at[3, half, low, :], s_x, r_x.at[p, 2], right)
        arrived(rows_x.at[2, half, rows, :], r_x.at[p, 1])
        send(rows_x.at[2, half, high, :], rows_x.at[3, half, high, :], s_x, r_x.at[p, 3], left)

    def all_here(p):
        block, half = source(p)
        arrived(rows_x.at[3, half, block_rows(block, HALF), :], r_x.at[p, 2])
        arrived(rows_x.at[3, half, block_rows(block, HALF, HALF), :], r_x.at[p, 3])

    def features(slot, half):
        shift = (0, 3, 1, 2)[slot] if isinstance(slot, int) else jnp.where(
            slot == 0, 0, jnp.where(slot == 1, 3, slot - 1)
        )
        return pl.ds(pl.multiple_of((lax.rem(x + shift, NX) * ZH + half) * FS, FS), FS)

    def compute(p):
        q = p - ZL
        block, _ = source(p)
        rows = block_rows(block)
        a = jnp.zeros((TOK, HID), F32)
        u = jnp.zeros((TOK, HID), F32)
        g = jnp.zeros((TOK, HID), F32)
        for slot in range(NX):
            for half in range(ZH):
                f = features(slot, half)
                xs = rows_x[slot, half, rows, 0:FS]
                dys = rows_x[slot, half, rows, FS:WIDE]
                a = a + dot(xs, wg[:, f], 1, 1)
                u = u + dot(xs, wu[:, f], 1, 1)
                g = g + dot(dys, wd[:, f], 1, 1)
        weight = wrow[rows, :].astype(F32)[:, 0:1]
        sig = jax.nn.sigmoid(a)
        act = a * sig
        hidden = (act * u).astype(BF16).astype(F32)
        dp = jnp.sum((hidden * g).T, axis=0, keepdims=True)
        dpx[q, x] = jnp.broadcast_to(dp, (8, TOK))
        for d in range(1, NX):
            send(dpx.at[q, x], dpx.at[q, x], s_d, r_d.at[q], {"x": lax.rem(x + d, NX)})
        dh = weight * g
        d_a = dh * u * sig * (1.0 + a * (1.0 - sig))
        d_u = dh * act
        lanes = pl.ds(pl.multiple_of(block * TOK, TOK), TOK)
        dau_t[0:HID, lanes] = d_a.T.astype(BF16)
        dau_t[HID : 2 * HID, lanes] = d_u.T.astype(BF16)
        ph_t[:, lanes] = (weight * hidden).T.astype(BF16)
        d_a = d_a.astype(BF16)
        d_u = d_u.astype(BF16)
        for slot in (3, 2, 1, 0):
            for half in range(ZH):
                f = features(slot, half)
                to = slice(half * FS, half * FS + FS)
                term = dot(d_a, wg[:, f]) + dot(d_u, wu[:, f])
                if slot == 0:
                    own[q, :, to] = term
                elif slot == 3:
                    part_o[q, :, to] = term.astype(BF16)
                else:
                    part_rl[2 - slot, q, :, to] = term.astype(BF16)
            if slot == 3:
                send(part_o.at[q, pl.ds(0, HALF), :], buf_a.at[0, q], s_a, r_a.at[q, 0], right)
                send(part_o.at[q, pl.ds(HALF, HALF), :], buf_a.at[1, q], s_a, r_a.at[q, 1], left)

    def add_relay(p):
        q = p - ZL
        arrived(buf_a.at[0, q], r_a.at[q, 0])
        part_rl[0, q, 0:HALF, :] = (
            part_rl[0, q, 0:HALF, :].astype(F32) + buf_a[0, q].astype(F32)
        ).astype(BF16)
        send(part_rl.at[0, q], buf_b.at[0, q], s_b, r_b.at[q, 0], right)
        arrived(buf_a.at[1, q], r_a.at[q, 1])
        part_rl[1, q, HALF:TOK, :] = (
            part_rl[1, q, HALF:TOK, :].astype(F32) + buf_a[1, q].astype(F32)
        ).astype(BF16)
        send(part_rl.at[1, q], buf_b.at[1, q], s_b, r_b.at[q, 1], left)

    def send_back(p):
        q = p - ZL
        arrived(dpx.at[q, pl.ds(0, NX - 1)], r_d.at[q])
        dp = (dpx[q, 0] + dpx[q, 1]) + (dpx[q, 2] + dpx[q, 3])
        fsend[q, :, WIDE : WIDE + TOK] = jnp.broadcast_to(dp[0:1], (TOK, TOK)).T.astype(BF16)
        arrived(buf_b.at[0, q], r_b.at[q, 0])
        arrived(buf_b.at[1, q], r_b.at[q, 1])
        fsend[q, :, 0:WIDE] = (
            own[q] + buf_b[0, q].astype(F32) + buf_b[1, q].astype(F32)
        ).astype(BF16)
        my_rows = pl.ds(pl.multiple_of(me * CAP, CAP), CAP)
        frecv[q, my_rows, :] = fsend[q, my_rows, :]
        for d in FAR_FIRST:
            to = lax.rem(me + d, YC)
            theirs = pl.ds(pl.multiple_of(to * CAP, CAP), CAP)
            send(fsend.at[q, theirs, :], frecv.at[q, my_rows, :], s_f, r_f.at[q], at_yc(to))

    def combine(p, m):
        q = p - ZL
        block, far = source(p)
        near = 1 - far
        arrived(fsend.at[q, pl.ds(0, TOK - CAP), :], r_f.at[q])
        code, _ = routing(p)
        pick = spread(code, None).astype(BF16)
        gsend[q, :, 0:TOK, :] = jnp.stack(
            [dot(pick, frecv[q, :, h * FS : h * FS + FS], 0, 0) for h in range(ZH)]
        ).astype(BF16)
        dp = frecv[q, :, WIDE : WIDE + TOK].astype(F32)
        dp_rows = jnp.zeros((META, TOK), F32)
        for k in range(TOP):
            one = jnp.sum(jnp.where(row_f == code[k : k + 1], dp, 0.0), axis=0, keepdims=True)
            dp_rows = jnp.where(line == k, one, dp_rows)
        for half in range(ZH):
            gsend[q, half, TOK : TOK + META, 0:TOK] = dp_rows.astype(BF16)
            gsend[q, half, TOK : TOK + META, TOK : 2 * TOK] = jnp.zeros((META, TOK), BF16)

        def place(to):
            away = lax.rem(to + NZ - z, NZ)
            return jnp.where(away < 5, away, away - 7)

        @pl.when((m >= 2) & (m < 7))
        def _():
            arrived(chain.at[m], r_c.at[m])
            gsend[q, far] = (gsend[q, far].astype(F32) + chain[m].astype(F32)).astype(BF16)

        @pl.when(m == 7)
        def _():
            for n, half in ((8, far), (7, near)):
                arrived(chain.at[n], r_c.at[n])
                gsend[q, half] = (gsend[q, half].astype(F32) + chain[n].astype(F32)).astype(BF16)

        @pl.when(m < 7)
        def _():
            step = jnp.where(lax.rem(m, 2) == 0, 1, NZ - 1)
            send(gsend.at[q, far], chain.at[m + 2], s_c, r_c.at[m + 2], at_z(lax.rem(z + step, NZ)))

        @pl.when(m == 7)
        def _():
            to = block + far * ZL
            send(gsend.at[q, far], zrecv.at[place(to)], s_g, r_g, at_z(to))

        @pl.when(m > 0)
        def _():
            to = block + near * ZL
            send(gsend.at[q, near], zrecv.at[place(to)], s_g, r_g, at_z(to))

        @pl.when(m == 0)
        def _():
            zrecv[0] = gsend[q, near]

    def weight_grads(slot):
        for half in range(ZH):
            f = features(slot, half)
            both = dot(dau_t[...], rows_x[slot, half, :, 0:FS])
            ggate[:, f] = both[0:HID].astype(BF16)
            gup[:, f] = both[HID : 2 * HID].astype(BF16)
            gdown[:, f] = dot(ph_t[...], rows_x[slot, half, :, FS:WIDE]).astype(BF16)

    def turn(j):
        m = j - ZL
        late = jnp.where(lax.rem(j, 2) == 1, jnp.maximum(14 - m, ZL), jnp.minimum(NZ - m, NZ - 1))
        return jnp.where(j < ZL, j, late)

    def step(i, carry):
        def when(lag, least, act):
            j = i - lag

            @pl.when((j >= least) & (j < NZ))
            def _():
                act(turn(j), *((j - ZL,) if act is combine else ()))

        @pl.when((i > 0) & (i <= ZL))
        def _():
            take_in(2 * i - 1)

        @pl.when(i < ZL)
        def _():
            take_in(2 * i)

        when(1, 0, pass_on)

        @pl.when((i < 2) | (i == ZL))
        def _():
            pack(turn(i))

        @pl.when((i > 0) & (i != ZL - 1) & (i < NZ - 1))
        def _():
            pack(turn(i + 1))

        when(2, 0, relay)
        when(6, ZL, combine)
        when(5, ZL, send_back)
        when(4, ZL, add_relay)
        when(3, 0, all_here)

        @pl.when(i == ZL)
        def _():
            for load in loads:
                load.wait()

        when(3, ZL, compute)

        @pl.when(i >= NZ + 2)
        def _():
            weight_grads(i - (NZ + 2))

        return carry

    lax.fori_loop(0, NZ + 6, step, 0)
    for store in stores:
        store.start()

    arrived(zrecv.at[pl.ds(1, SUMS - 1)], r_g)
    total = jnp.zeros((TOK, FS), F32)
    dp = jnp.zeros((META, TOK), F32)
    for s in range(SUMS):
        total = total + zrecv[s, 0:TOK, :].astype(F32)
        dp = dp + zrecv[s, TOK : TOK + META, 0:TOK].astype(F32)
    gtok[...] = total.astype(BF16)
    gprob[...] = dp[0:TOP].astype(BF16)
    for store in stores:
        store.wait()

    arrived(held.at[pl.ds(0, ZL - 1)], s_z.at[0])
    arrived(held.at[pl.ds(0, ZL), pl.ds(0, TOK)], s_z.at[1])
    arrived(ysend.at[:, pl.ds(0, TOK - CAP), :], s_y)
    arrived(wsend.at[:, pl.ds(0, TOK - CAP), :], s_w)
    arrived(rows_x.at[pl.ds(1, NX - 1)], s_x)
    arrived(part_o, s_a)
    arrived(part_rl, s_b)
    arrived(fsend.at[:, pl.ds(0, TOK - CAP), :], s_f)
    arrived(zrecv.at[pl.ds(1, SUMS - 1)], s_g)
    arrived(chain.at[pl.ds(2, 7)], s_c)
    arrived(dpx.at[:, pl.ds(0, NX - 1)], s_d)


def hand_over(*refs):
    far, out, near, sems = refs[:5], refs[5:10], refs[10:15], refs[15]
    loads = [pltpu.make_async_copy(far[n], near[n], sems.at[0, n]) for n in range(5)]
    stores = [pltpu.make_async_copy(near[n], out[n], sems.at[1, n]) for n in range(5)]
    for load in loads:
        load.start()
    for load, store in zip(loads, stores):
        load.wait()
        store.start()
    for store in stores:
        store.wait()


def body(tokens, upstream, probs, expert_ids, gate_weight, up_weight, down_weight):
    vmem = pl.BlockSpec(memory_space=pltpu.VMEM)
    anywhere = pl.BlockSpec(memory_space=pl.ANY)
    dma = pltpu.SemaphoreType.DMA
    width = NX * ZH * FS
    out = (
        jax.ShapeDtypeStruct((TOK, FS), BF16),
        jax.ShapeDtypeStruct((TOP, TOK), BF16),
    ) + (jax.ShapeDtypeStruct((1, HID, width), BF16),) * 3
    results = pl.pallas_call(
        kernel,
        out_shape=out,
        in_specs=[vmem] * 4 + [anywhere] * 3,
        out_specs=(vmem,) * 2 + (anywhere,) * 3,
        scratch_shapes=[pltpu.VMEM((HID, width), BF16)] * 6
        + [
            dma((3,)), dma((3,)),
            pltpu.VMEM((NZ, TOK + META, WIDE), BF16),
            pltpu.VMEM((NZ, TOK, WIDE), BF16),
            pltpu.VMEM((ZL, TOK, TOK), BF16),
            pltpu.VMEM((NX, ZH, ZL * TOK, WIDE), BF16),
            pltpu.VMEM((ZL * TOK, TOK), BF16),
            pltpu.VMEM((2 * HID, ZL * TOK), BF16),
            pltpu.VMEM((HID, ZL * TOK), BF16),
            pltpu.VMEM((ZL, TOK, WIDE), F32),
            pltpu.VMEM((ZL, TOK, WIDE), BF16),
            pltpu.VMEM((2, ZL, TOK, WIDE), BF16),
            pltpu.VMEM((2, ZL, HALF, WIDE), BF16),
            pltpu.VMEM((2, ZL, TOK, WIDE), BF16),
            pltpu.VMEM((ZL, TOK, WIDE + TOK), BF16),
            pltpu.VMEM((ZL, TOK, WIDE + TOK), BF16),
            pltpu.VMEM((ZL, ZH, TOK + META, FS), BF16),
            pltpu.VMEM((SUMS, TOK + META, FS), BF16),
            pltpu.VMEM((9, TOK + META, FS), BF16),
            pltpu.VMEM((ZL, NX, 8, TOK), F32),
            dma((2,)), dma((NZ,)),
            dma, dma((NZ,)),
            dma, dma((ZL,)),
            dma, dma((NZ, 4)),
            dma, dma((ZL, 2)),
            dma, dma((ZL, 2)),
            dma, dma((ZL,)),
            dma, dma((9,)),
            dma, dma,
            dma, dma((ZL,)),
        ],
        compiler_params=pltpu.CompilerParams(
            collective_id=0, has_side_effects=True, vmem_limit_bytes=56 * 1024 * 1024
        ),
        cost_estimate=pl.CostEstimate(
            flops=16 * ZL * TOK * HID * width, bytes_accessed=8 << 20, transcendentals=0
        ),
    )(tokens, upstream, probs.T, expert_ids.T, gate_weight, up_weight, down_weight)
    tokens_out, probs_out, *weights_out = pl.pallas_call(
        hand_over,
        out_shape=out,
        in_specs=[anywhere] * 5,
        out_specs=(anywhere,) * 5,
        scratch_shapes=[pltpu.VMEM(o.shape, o.dtype) for o in out] + [dma((2, 5))],
    )(*results)
    return (tokens_out, probs_out.T, *weights_out)


def solution(mesh):
    parts = Mesh(mesh.devices.reshape(ZL, NY, NC, NX, ZH), ("zl", "y", "c", "x", "zh"))
    expert, tensor = ("zl", "y", "c"), ("x", "zh")
    placed = (
        P(expert, tensor),
        P(expert, tensor),
        P(expert, None),
        P(expert, None),
        P(expert, tensor, None),
        P(expert, tensor, None),
        P(expert, tensor, None),
    )
    return jax.shard_map(
        body,
        mesh=parts,
        in_specs=placed,
        out_specs=(
            P(expert, tensor),
            P(expert, None),
            P(expert, tensor, None),
            P(expert, tensor, None),
            P(expert, tensor, None),
        ),
        check_vma=False,
    )
```

```python
import jax
import jax.numpy as jnp
from jax import lax
from jax.experimental import pallas as pl
from jax.experimental.pallas import tpu as pltpu
from jax.sharding import Mesh
from jax.sharding import PartitionSpec as P

MESH = pl.DeviceIdType.MESH
F32 = jnp.float32
BF16 = jnp.bfloat16

ZL, NY, NC, NX, ZH = 8, 4, 2, 4, 2
NZ = ZL * ZH
YC = NY * NC
TOK = 128
TOP = 6
CAP = 16
FS = 256
HID = 176
META = 16
WIDE = 2 * FS
HALF = TOK // 2
FAR_FIRST = (4, 3, 5, 2, 6, 1, 7)
SUMS = 9


def dot(a, b, ad=1, bd=0):
    return lax.dot_general(a, b, (((ad,), (bd,)), ((), ())), preferred_element_type=F32)


def arrived(ref, sem):
    pltpu.make_async_copy(ref, ref, sem).wait()


def kernel(
    tok, ups, prob, ids, wg_far, wu_far, wd_far,
    gtok, gprob, ggate_far, gup_far, gdown_far,
    wg, wu, wd, ggate, gup, gdown, s_in, s_out,
    held, ysend, wsend, rows_x, wrow, dau_t, ph_t, own, part_o, part_rl, buf_a, buf_b,
    fsend, frecv, gsend, zrecv, chain, dpx,
    s_z, r_z, s_y, r_y, s_w, r_w, s_x, r_x, s_a, r_a, s_b, r_b, s_f, r_f, s_c, r_c, s_g, r_g, s_d, r_d,
):
    zl, zh = lax.axis_index("zl"), lax.axis_index("zh")
    x = lax.axis_index("x")
    me = lax.axis_index("y") * NC + lax.axis_index("c")
    z = zh * ZL + zl

    def at_z(place):
        return {"zl": lax.rem(place, ZL), "zh": lax.div(place, ZL)}

    def at_yc(place):
        return {"y": lax.div(place, NC), "c": lax.rem(place, NC)}

    right, left = {"x": lax.rem(x + 1, NX)}, {"x": lax.rem(x + 3, NX)}

    def send(src, dst, s_sem, r_sem, device):
        pltpu.make_async_remote_copy(
            src_ref=src, dst_ref=dst, send_sem=s_sem, recv_sem=r_sem,
            device_id=device, device_id_type=MESH,
        ).start()

    loads = [
        pltpu.make_async_copy(far.at[0], near, s_in.at[n])
        for n, (far, near) in enumerate(((wg_far, wg), (wu_far, wu), (wd_far, wd)))
    ]
    stores = [
        pltpu.make_async_copy(near, far.at[0], s_out.at[n])
        for n, (near, far) in enumerate(((ggate, ggate_far), (gup, gup_far), (gdown, gdown_far)))
    ]
    for load in loads:
        load.start()

    barrier = pltpu.get_barrier_semaphore()
    for d in range(1, NZ):
        pl.semaphore_signal(barrier, inc=1, device_id=at_z(lax.rem(z + d, NZ)), device_id_type=MESH)
    for d in range(1, YC):
        pl.semaphore_signal(barrier, inc=1, device_id=at_yc(lax.rem(me + d, YC)), device_id_type=MESH)
    for d in range(1, NX):
        pl.semaphore_signal(barrier, inc=1, device_id={"x": lax.rem(x + d, NX)}, device_id_type=MESH)

    row_id = lax.broadcasted_iota(jnp.int32, (TOK, TOK), 0)
    col_id = lax.broadcasted_iota(jnp.int32, (TOK, TOK), 1)
    earlier = (row_id < col_id).astype(F32).astype(BF16)
    held[0, 0:TOK, 0:FS] = tok[...]
    held[0, 0:TOK, FS:WIDE] = ups[...]
    ids_t = ids[...].astype(F32)
    prob_t = prob[...].astype(F32)
    expert = lax.broadcasted_iota(jnp.int32, (ZL * YC, TOK), 0).astype(F32)
    named = jnp.zeros((ZL * YC, TOK), F32)
    for k in range(TOP):
        named = named + jnp.where(ids_t[k : k + 1] == expert, 1.0, 0.0)
    before = dot(named.astype(BF16), earlier)
    line = lax.broadcasted_iota(jnp.int32, (META, TOK), 0)
    id_rows = jnp.zeros((META, TOK), F32)
    slot_rows = jnp.zeros((META, TOK), F32)
    prob_rows = jnp.zeros((META, TOK), F32)
    for k in range(TOP):
        slot = jnp.sum(jnp.where(ids_t[k : k + 1] == expert, before, 0.0), axis=0, keepdims=True)
        id_rows = jnp.where(line == k, ids_t[k : k + 1], id_rows)
        slot_rows = jnp.where(line == k, slot, slot_rows)
        prob_rows = jnp.where(line == k, prob_t[k : k + 1], prob_rows)
    held[0, TOK : TOK + META, 0:TOK] = id_rows.astype(BF16)
    held[0, TOK : TOK + META, TOK : 2 * TOK] = slot_rows.astype(BF16)
    held[0, TOK : TOK + META, 2 * TOK : 3 * TOK] = prob_rows.astype(BF16)
    held[0, TOK : TOK + META, 3 * TOK : 4 * TOK] = jnp.zeros((META, TOK), BF16)

    pl.semaphore_wait(barrier, NZ + YC + NX - 3)

    def source(p):
        odd = lax.rem(p, 2) == 1
        place = lax.rem(z + jnp.where(odd, NZ - lax.div(p + 1, 2), lax.div(p, 2)), NZ)
        return lax.rem(place, ZL), lax.div(place, ZL)

    def block_rows(block, count=TOK, extra=0):
        return pl.ds(pl.multiple_of(block * TOK + extra, CAP), count)

    row_f = row_id.astype(F32)

    def routing(p):
        first = jnp.where(p < ZL, p, NZ - 1 - p)
        meta = held[first, TOK : TOK + META, :].astype(F32)
        code = (meta[:, 0:TOK] - (zl * YC).astype(F32)) * CAP + meta[:, TOK : 2 * TOK]
        return code, meta[:, 2 * TOK : 3 * TOK]

    def spread(code, values):
        total = jnp.zeros((TOK, TOK), F32)
        for k in range(TOP):
            value = 1.0 if values is None else values[k : k + 1]
            total = total + jnp.where(row_f == code[k : k + 1], value, 0.0)
        return total

    def top(p):
        return held.at[p, pl.ds(0, HALF)]

    def rest(p, rows):
        return held.at[p, pl.ds(HALF, rows)]

    routed, bare = HALF + META, HALF

    def onward(p):
        return at_z(lax.rem(z + jnp.where(lax.rem(p, 2) == 1, 1, NZ - 1), NZ))

    def take_top(p):
        arrived(top(p), r_z.at[p, 0])

        @pl.when(p < NZ - 2)
        def _():
            send(top(p), top(p + 2), s_z.at[0], r_z.at[p + 2, 0], onward(p))

    def take_rest(p):
        @pl.when(p < ZL)
        def _():
            arrived(rest(p, routed), r_z.at[p, 1])

        @pl.when(p >= ZL)
        def _():
            arrived(rest(p, bare), r_z.at[p, 1])

        @pl.when(p < ZL - 2)
        def _():
            send(rest(p, routed), rest(p + 2, routed), s_z.at[1], r_z.at[p + 2, 1], onward(p))

        @pl.when((p >= ZL - 2) & (p < NZ - 2))
        def _():
            send(rest(p, bare), rest(p + 2, bare), s_z.at[2], r_z.at[p + 2, 1], onward(p))

    def begin():
        for p, place in ((1, z + 1), (2, z + NZ - 1)):
            send(top(0), top(p), s_z.at[0], r_z.at[p, 0], at_z(lax.rem(place, NZ)))
        for p, place in ((1, z + 1), (2, z + NZ - 1)):
            send(rest(0, routed), rest(p, routed), s_z.at[1], r_z.at[p, 1], at_z(lax.rem(place, NZ)))

    def pack(p):
        block, half = source(p)
        code, weights = routing(p)
        pick = spread(code, None).astype(BF16)
        ysend[p] = dot(pick, held[p, 0:TOK, :]).astype(BF16)
        mine = block_rows(block, CAP, me * CAP)
        my_rows = pl.ds(pl.multiple_of(me * CAP, CAP), CAP)
        rows_x[0, half, mine, :] = ysend[p, my_rows, :]
        for d in FAR_FIRST:
            to = lax.rem(me + d, YC)
            theirs = pl.ds(pl.multiple_of(to * CAP, CAP), CAP)
            send(ysend.at[p, theirs, :], rows_x.at[0, half, mine, :], s_y, r_y.at[p], at_yc(to))

        @pl.when(p >= ZL)
        def _():
            q = p - ZL
            weight = jnp.sum(spread(code, weights), axis=1, keepdims=True)
            wsend[q] = jnp.broadcast_to(weight, (TOK, TOK)).astype(BF16)
            wrow[mine, :] = wsend[q, my_rows, :]
            for d in FAR_FIRST:
                to = lax.rem(me + d, YC)
                theirs = pl.ds(pl.multiple_of(to * CAP, CAP), CAP)
                send(wsend.at[q, theirs, :], wrow.at[mine, :], s_w, r_w.at[q], at_yc(to))

    def pass_on(p):
        block, half = source(p)
        rows = block_rows(block)
        arrived(ysend.at[p, pl.ds(0, TOK - CAP), :], r_y.at[p])

        @pl.when(p >= ZL)
        def _():
            arrived(wsend.at[p - ZL, pl.ds(0, TOK - CAP), :], r_w.at[p - ZL])

        send(rows_x.at[0, half, rows, :], rows_x.at[1, half, rows, :], s_x, r_x.at[p, 0], right)
        send(rows_x.at[0, half, rows, :], rows_x.at[2, half, rows, :], s_x, r_x.at[p, 1], left)

    def relay(p):
        block, half = source(p)
        rows = block_rows(block)
        low, high = block_rows(block, HALF), block_rows(block, HALF, HALF)
        arrived(rows_x.at[1, half, rows, :], r_x.at[p, 0])
        send(rows_x.at[1, half, low, :], rows_x.at[3, half, low, :], s_x, r_x.at[p, 2], right)
        arrived(rows_x.at[2, half, rows, :], r_x.at[p, 1])
        send(rows_x.at[2, half, high, :], rows_x.at[3, half, high, :], s_x, r_x.at[p, 3], left)

    def all_here(p):
        block, half = source(p)
        arrived(rows_x.at[3, half, block_rows(block, HALF), :], r_x.at[p, 2])
        arrived(rows_x.at[3, half, block_rows(block, HALF, HALF), :], r_x.at[p, 3])

    def features(slot, half):
        shift = (0, 3, 1, 2)[slot] if isinstance(slot, int) else jnp.where(
            slot == 0, 0, jnp.where(slot == 1, 3, slot - 1)
        )
        return pl.ds(pl.multiple_of((lax.rem(x + shift, NX) * ZH + half) * FS, FS), FS)

    def compute(p):
        q = p - ZL
        block, _ = source(p)
        rows = block_rows(block)
        a = jnp.zeros((TOK, HID), F32)
        u = jnp.zeros((TOK, HID), F32)
        g = jnp.zeros((TOK, HID), F32)
        for slot in range(NX):
            for half in range(ZH):
                f = features(slot, half)
                xs = rows_x[slot, half, rows, 0:FS]
                dys = rows_x[slot, half, rows, FS:WIDE]
                a = a + dot(xs, wg[:, f], 1, 1)
                u = u + dot(xs, wu[:, f], 1, 1)
                g = g + dot(dys, wd[:, f], 1, 1)
        weight = wrow[rows, :].astype(F32)[:, 0:1]
        sig = jax.nn.sigmoid(a)
        act = a * sig
        hidden = (act * u).astype(BF16).astype(F32)
        dp = jnp.sum((hidden * g).T, axis=0, keepdims=True)
        dpx[q, x] = jnp.broadcast_to(dp, (8, TOK))
        for d in range(1, NX):
            send(dpx.at[q, x], dpx.at[q, x], s_d, r_d.at[q], {"x": lax.rem(x + d, NX)})
        dh = weight * g
        d_a = dh * u * sig * (1.0 + a * (1.0 - sig))
        d_u = dh * act
        lanes = pl.ds(pl.multiple_of(block * TOK, TOK), TOK)
        dau_t[0:HID, lanes] = d_a.T.astype(BF16)
        dau_t[HID : 2 * HID, lanes] = d_u.T.astype(BF16)
        ph_t[:, lanes] = (weight * hidden).T.astype(BF16)
        d_a = d_a.astype(BF16)
        d_u = d_u.astype(BF16)
        for slot in (3, 2, 1, 0):
            for half in range(ZH):
                f = features(slot, half)
                to = slice(half * FS, half * FS + FS)
                term = dot(d_a, wg[:, f]) + dot(d_u, wu[:, f])
                if slot == 0:
                    own[q, :, to] = term
                elif slot == 3:
                    part_o[q, :, to] = term.astype(BF16)
                else:
                    part_rl[2 - slot, q, :, to] = term.astype(BF16)
            if slot == 3:
                send(part_o.at[q, pl.ds(0, HALF), :], buf_a.at[0, q], s_a, r_a.at[q, 0], right)
                send(part_o.at[q, pl.ds(HALF, HALF), :], buf_a.at[1, q], s_a, r_a.at[q, 1], left)

    def add_relay(p):
        q = p - ZL
        arrived(buf_a.at[0, q], r_a.at[q, 0])
        part_rl[0, q, 0:HALF, :] = (
            part_rl[0, q, 0:HALF, :].astype(F32) + buf_a[0, q].astype(F32)
        ).astype(BF16)
        send(part_rl.at[0, q], buf_b.at[0, q], s_b, r_b.at[q, 0], right)
        arrived(buf_a.at[1, q], r_a.at[q, 1])
        part_rl[1, q, HALF:TOK, :] = (
            part_rl[1, q, HALF:TOK, :].astype(F32) + buf_a[1, q].astype(F32)
        ).astype(BF16)
        send(part_rl.at[1, q], buf_b.at[1, q], s_b, r_b.at[q, 1], left)

    def send_back(p):
        q = p - ZL
        arrived(dpx.at[q, pl.ds(0, NX - 1)], r_d.at[q])
        dp = (dpx[q, 0] + dpx[q, 1]) + (dpx[q, 2] + dpx[q, 3])
        fsend[q, :, WIDE : WIDE + TOK] = jnp.broadcast_to(dp[0:1], (TOK, TOK)).T.astype(BF16)
        arrived(buf_b.at[0, q], r_b.at[q, 0])
        arrived(buf_b.at[1, q], r_b.at[q, 1])
        fsend[q, :, 0:WIDE] = (
            own[q] + buf_b[0, q].astype(F32) + buf_b[1, q].astype(F32)
        ).astype(BF16)
        my_rows = pl.ds(pl.multiple_of(me * CAP, CAP), CAP)
        frecv[q, my_rows, :] = fsend[q, my_rows, :]
        for d in FAR_FIRST:
            to = lax.rem(me + d, YC)
            theirs = pl.ds(pl.multiple_of(to * CAP, CAP), CAP)
            send(fsend.at[q, theirs, :], frecv.at[q, my_rows, :], s_f, r_f.at[q], at_yc(to))

    def combine(p, m):
        q = p - ZL
        block, far = source(p)
        near = 1 - far
        arrived(fsend.at[q, pl.ds(0, TOK - CAP), :], r_f.at[q])
        code, _ = routing(p)
        pick = spread(code, None).astype(BF16)
        dp = frecv[q, :, WIDE : WIDE + TOK].astype(F32)
        dp_rows = jnp.zeros((META, TOK), F32)
        for k in range(TOP):
            one = jnp.sum(jnp.where(row_f == code[k : k + 1], dp, 0.0), axis=0, keepdims=True)
            dp_rows = jnp.where(line == k, one, dp_rows)

        def gather(half):
            features_of = pl.ds(pl.multiple_of(half * FS, FS), FS)
            gsend[q, half, 0:TOK, :] = dot(pick, frecv[q, :, features_of], 0, 0).astype(BF16)
            gsend[q, half, TOK : TOK + META, 0:TOK] = dp_rows.astype(BF16)
            gsend[q, half, TOK : TOK + META, TOK : 2 * TOK] = jnp.zeros((META, TOK), BF16)

        gather(far)

        def place(to):
            away = lax.rem(to + NZ - z, NZ)
            return jnp.where(away < 5, away, away - 7)

        def add(half, n):
            arrived(chain.at[n], r_c.at[n])
            gsend[q, half] = (gsend[q, half].astype(F32) + chain[n].astype(F32)).astype(BF16)

        @pl.when((m >= 2) & (m < 7))
        def _():
            add(far, m)

        @pl.when(m < 7)
        def _():
            step = jnp.where(lax.rem(m, 2) == 0, 1, NZ - 1)
            send(gsend.at[q, far], chain.at[m + 2], s_c, r_c.at[m + 2], at_z(lax.rem(z + step, NZ)))

        @pl.when(m == 7)
        def _():
            add(far, 8)
            to = block + far * ZL
            send(gsend.at[q, far], zrecv.at[place(to)], s_g, r_g, at_z(to))

        gather(near)

        @pl.when(m == 7)
        def _():
            add(near, 7)

        @pl.when(m > 0)
        def _():
            to = block + near * ZL
            send(gsend.at[q, near], zrecv.at[place(to)], s_g, r_g, at_z(to))

        @pl.when(m == 0)
        def _():
            zrecv[0] = gsend[q, near]

    def weight_grads(slot):
        for half in range(ZH):
            f = features(slot, half)
            both = dot(dau_t[...], rows_x[slot, half, :, 0:FS])
            ggate[:, f] = both[0:HID].astype(BF16)
            gup[:, f] = both[HID : 2 * HID].astype(BF16)
            gdown[:, f] = dot(ph_t[...], rows_x[slot, half, :, FS:WIDE]).astype(BF16)

    def rank(j):
        m = j - ZL
        return jnp.where(m < 2, 1 - m, m)

    def turn(j):
        m = rank(j)
        late = jnp.where(lax.rem(j, 2) == 1, jnp.maximum(14 - m, ZL), jnp.minimum(NZ - m, NZ - 1))
        late = jnp.where(m == 0, NZ - 1, jnp.where(m == 1, NZ - 3, late))
        return jnp.where(j < ZL, j, late)

    def step(i, carry):
        def when(lag, least, act):
            j = i - lag

            @pl.when((j >= least) & (j < NZ))
            def _():
                act(turn(j), *((rank(j),) if act is combine else ()))

        def both(act):
            @pl.when((i > 0) & (i <= ZL))
            def _():
                act(2 * i - 1)

            @pl.when((i > 0) & (i < ZL))
            def _():
                act(2 * i)

        both(take_top)
        when(6, ZL, combine)
        when(1, 0, pass_on)
        both(take_rest)

        @pl.when(i < 2)
        def _():
            pack(turn(i))

        @pl.when((i > 0) & (i < NZ - 1))
        def _():
            pack(turn(i + 1))

        when(5, ZL, send_back)
        when(2, 0, relay)
        when(4, ZL, add_relay)
        when(3, 0, all_here)

        @pl.when(i == ZL)
        def _():
            for load in loads:
                load.wait()

        when(3, ZL, compute)

        @pl.when(i >= NZ + 2)
        def _():
            weight_grads(i - (NZ + 2))

        return carry

    begin()
    lax.fori_loop(0, NZ + 6, step, 0)
    for store in stores:
        store.start()

    arrived(zrecv.at[pl.ds(1, SUMS - 1)], r_g)
    total = jnp.zeros((TOK, FS), F32)
    dp = jnp.zeros((META, TOK), F32)
    for s in range(SUMS):
        total = total + zrecv[s, 0:TOK, :].astype(F32)
        dp = dp + zrecv[s, TOK : TOK + META, 0:TOK].astype(F32)
    gtok[...] = total.astype(BF16)
    gprob[...] = dp[0:TOP].astype(BF16)
    for store in stores:
        store.wait()

    arrived(held.at[pl.ds(0, NZ - 1), pl.ds(0, HALF)], s_z.at[0])
    arrived(held.at[pl.ds(0, ZL - 1), pl.ds(HALF, routed)], s_z.at[1])
    arrived(held.at[pl.ds(0, ZL), pl.ds(HALF, bare)], s_z.at[2])
    arrived(ysend.at[:, pl.ds(0, TOK - CAP), :], s_y)
    arrived(wsend.at[:, pl.ds(0, TOK - CAP), :], s_w)
    arrived(rows_x.at[pl.ds(1, NX - 1)], s_x)
    arrived(part_o, s_a)
    arrived(part_rl, s_b)
    arrived(fsend.at[:, pl.ds(0, TOK - CAP), :], s_f)
    arrived(zrecv.at[pl.ds(1, SUMS - 1)], s_g)
    arrived(chain.at[pl.ds(2, 7)], s_c)
    arrived(dpx.at[:, pl.ds(0, NX - 1)], s_d)


def hand_over(*refs):
    far, out, near, sems = refs[:5], refs[5:10], refs[10:15], refs[15]
    loads = [pltpu.make_async_copy(far[n], near[n], sems.at[0, n]) for n in range(5)]
    stores = [pltpu.make_async_copy(near[n], out[n], sems.at[1, n]) for n in range(5)]
    for load in loads:
        load.start()
    for load, store in zip(loads, stores):
        load.wait()
        store.start()
    for store in stores:
        store.wait()


def body(tokens, upstream, probs, expert_ids, gate_weight, up_weight, down_weight):
    vmem = pl.BlockSpec(memory_space=pltpu.VMEM)
    anywhere = pl.BlockSpec(memory_space=pl.ANY)
    dma = pltpu.SemaphoreType.DMA
    width = NX * ZH * FS
    out = (
        jax.ShapeDtypeStruct((TOK, FS), BF16),
        jax.ShapeDtypeStruct((TOP, TOK), BF16),
    ) + (jax.ShapeDtypeStruct((1, HID, width), BF16),) * 3
    results = pl.pallas_call(
        kernel,
        out_shape=out,
        in_specs=[vmem] * 4 + [anywhere] * 3,
        out_specs=(vmem,) * 2 + (anywhere,) * 3,
        scratch_shapes=[pltpu.VMEM((HID, width), BF16)] * 6
        + [
            dma((3,)), dma((3,)),
            pltpu.VMEM((NZ, TOK + META, WIDE), BF16),
            pltpu.VMEM((NZ, TOK, WIDE), BF16),
            pltpu.VMEM((ZL, TOK, TOK), BF16),
            pltpu.VMEM((NX, ZH, ZL * TOK, WIDE), BF16),
            pltpu.VMEM((ZL * TOK, TOK), BF16),
            pltpu.VMEM((2 * HID, ZL * TOK), BF16),
            pltpu.VMEM((HID, ZL * TOK), BF16),
            pltpu.VMEM((ZL, TOK, WIDE), F32),
            pltpu.VMEM((ZL, TOK, WIDE), BF16),
            pltpu.VMEM((2, ZL, TOK, WIDE), BF16),
            pltpu.VMEM((2, ZL, HALF, WIDE), BF16),
            pltpu.VMEM((2, ZL, TOK, WIDE), BF16),
            pltpu.VMEM((ZL, TOK, WIDE + TOK), BF16),
            pltpu.VMEM((ZL, TOK, WIDE + TOK), BF16),
            pltpu.VMEM((ZL, ZH, TOK + META, FS), BF16),
            pltpu.VMEM((SUMS, TOK + META, FS), BF16),
            pltpu.VMEM((9, TOK + META, FS), BF16),
            pltpu.VMEM((ZL, NX, 8, TOK), F32),
            dma((3,)), dma((NZ, 2)),
            dma, dma((NZ,)),
            dma, dma((ZL,)),
            dma, dma((NZ, 4)),
            dma, dma((ZL, 2)),
            dma, dma((ZL, 2)),
            dma, dma((ZL,)),
            dma, dma((9,)),
            dma, dma,
            dma, dma((ZL,)),
        ],
        compiler_params=pltpu.CompilerParams(
            collective_id=0, has_side_effects=True, vmem_limit_bytes=56 * 1024 * 1024
        ),
        cost_estimate=pl.CostEstimate(
            flops=16 * ZL * TOK * HID * width, bytes_accessed=8 << 20, transcendentals=0
        ),
    )(tokens, upstream, probs.T, expert_ids.T, gate_weight, up_weight, down_weight)
    tokens_out, probs_out, *weights_out = pl.pallas_call(
        hand_over,
        out_shape=out,
        in_specs=[anywhere] * 5,
        out_specs=(anywhere,) * 5,
        scratch_shapes=[pltpu.VMEM(o.shape, o.dtype) for o in out] + [dma((2, 5))],
    )(*results)
    return (tokens_out, probs_out.T, *weights_out)


def solution(mesh):
    parts = Mesh(mesh.devices.reshape(ZL, NY, NC, NX, ZH), ("zl", "y", "c", "x", "zh"))
    expert, tensor = ("zl", "y", "c"), ("x", "zh")
    placed = (
        P(expert, tensor),
        P(expert, tensor),
        P(expert, None),
        P(expert, None),
        P(expert, tensor, None),
        P(expert, tensor, None),
        P(expert, tensor, None),
    )
    return jax.shard_map(
        body,
        mesh=parts,
        in_specs=placed,
        out_specs=(
            P(expert, tensor),
            P(expert, None),
            P(expert, tensor, None),
            P(expert, tensor, None),
            P(expert, tensor, None),
        ),
        check_vma=False,
    )
```

```python
import jax
import jax.numpy as jnp
from jax import lax
from jax.experimental import pallas as pl
from jax.experimental.pallas import tpu as pltpu
from jax.sharding import Mesh
from jax.sharding import PartitionSpec as P

MESH = pl.DeviceIdType.MESH
F32 = jnp.float32
BF16 = jnp.bfloat16

ZL, NY, NC, NX, ZH = 8, 4, 2, 4, 2
NZ = ZL * ZH
YC = NY * NC
TOK = 128
TOP = 6
CAP = 16
FS = 256
HID = 176
META = 16
WIDE = 2 * FS
HALF = TOK // 2
FAR_FIRST = (4, 3, 5, 2, 6, 1, 7)
SUMS = 9


def dot(a, b, ad=1, bd=0):
    return lax.dot_general(a, b, (((ad,), (bd,)), ((), ())), preferred_element_type=F32)


def arrived(ref, sem):
    pltpu.make_async_copy(ref, ref, sem).wait()


def kernel(
    tok, ups, prob, ids, wg_far, wu_far, wd_far,
    gtok, gprob, ggate_far, gup_far, gdown_far,
    wg, wu, wd, ggate, gup, gdown, s_in, s_out,
    held, ysend, wsend, rows_x, wrow, dau_t, ph_t, own, part_o, part_rl, buf_a, buf_b,
    fsend, frecv, gsend, zrecv, chain, dpx,
    s_z, r_z, s_y, r_y, s_w, r_w, s_x, r_x, s_a, r_a, s_b, r_b, s_f, r_f, s_c, r_c, s_g, r_g, s_d, r_d,
):
    zl, zh = lax.axis_index("zl"), lax.axis_index("zh")
    x = lax.axis_index("x")
    me = lax.axis_index("y") * NC + lax.axis_index("c")
    z = zh * ZL + zl

    def at_z(place):
        return {"zl": lax.rem(place, ZL), "zh": lax.div(place, ZL)}

    def at_yc(place):
        return {"y": lax.div(place, NC), "c": lax.rem(place, NC)}

    right, left = {"x": lax.rem(x + 1, NX)}, {"x": lax.rem(x + 3, NX)}

    def send(src, dst, s_sem, r_sem, device):
        pltpu.make_async_remote_copy(
            src_ref=src, dst_ref=dst, send_sem=s_sem, recv_sem=r_sem,
            device_id=device, device_id_type=MESH,
        ).start()

    loads = [
        pltpu.make_async_copy(far.at[0], near, s_in.at[n])
        for n, (far, near) in enumerate(((wg_far, wg), (wu_far, wu), (wd_far, wd)))
    ]
    stores = [
        pltpu.make_async_copy(near, far.at[0], s_out.at[n])
        for n, (near, far) in enumerate(((ggate, ggate_far), (gup, gup_far), (gdown, gdown_far)))
    ]
    for load in loads:
        load.start()

    barrier = pltpu.get_barrier_semaphore()
    for d in range(1, NZ):
        pl.semaphore_signal(barrier, inc=1, device_id=at_z(lax.rem(z + d, NZ)), device_id_type=MESH)
    for d in range(1, YC):
        pl.semaphore_signal(barrier, inc=1, device_id=at_yc(lax.rem(me + d, YC)), device_id_type=MESH)
    for d in range(1, NX):
        pl.semaphore_signal(barrier, inc=1, device_id={"x": lax.rem(x + d, NX)}, device_id_type=MESH)

    row_id = lax.broadcasted_iota(jnp.int32, (TOK, TOK), 0)
    col_id = lax.broadcasted_iota(jnp.int32, (TOK, TOK), 1)
    earlier = (row_id < col_id).astype(F32).astype(BF16)
    held[0, 0:TOK, 0:FS] = tok[...]
    held[0, 0:TOK, FS:WIDE] = ups[...]
    ids_t = ids[...].astype(F32)
    prob_t = prob[...].astype(F32)
    expert = lax.broadcasted_iota(jnp.int32, (ZL * YC, TOK), 0).astype(F32)
    named = jnp.zeros((ZL * YC, TOK), F32)
    for k in range(TOP):
        named = named + jnp.where(ids_t[k : k + 1] == expert, 1.0, 0.0)
    before = dot(named.astype(BF16), earlier)
    line = lax.broadcasted_iota(jnp.int32, (META, TOK), 0)
    id_rows = jnp.zeros((META, TOK), F32)
    slot_rows = jnp.zeros((META, TOK), F32)
    prob_rows = jnp.zeros((META, TOK), F32)
    for k in range(TOP):
        slot = jnp.sum(jnp.where(ids_t[k : k + 1] == expert, before, 0.0), axis=0, keepdims=True)
        id_rows = jnp.where(line == k, ids_t[k : k + 1], id_rows)
        slot_rows = jnp.where(line == k, slot, slot_rows)
        prob_rows = jnp.where(line == k, prob_t[k : k + 1], prob_rows)
    held[0, TOK : TOK + META, 0:TOK] = id_rows.astype(BF16)
    held[0, TOK : TOK + META, TOK : 2 * TOK] = slot_rows.astype(BF16)
    held[0, TOK : TOK + META, 2 * TOK : 3 * TOK] = prob_rows.astype(BF16)
    held[0, TOK : TOK + META, 3 * TOK : 4 * TOK] = jnp.zeros((META, TOK), BF16)

    pl.semaphore_wait(barrier, NZ + YC + NX - 3)

    def source(p):
        odd = lax.rem(p, 2) == 1
        place = lax.rem(z + jnp.where(odd, NZ - lax.div(p + 1, 2), lax.div(p, 2)), NZ)
        return lax.rem(place, ZL), lax.div(place, ZL)

    def block_rows(block, count=TOK, extra=0):
        return pl.ds(pl.multiple_of(block * TOK + extra, CAP), count)

    row_f = row_id.astype(F32)

    def routing(p):
        first = jnp.where(p < ZL, p, NZ - 1 - p)
        meta = held[first, TOK : TOK + META, :].astype(F32)
        code = (meta[:, 0:TOK] - (zl * YC).astype(F32)) * CAP + meta[:, TOK : 2 * TOK]
        return code, meta[:, 2 * TOK : 3 * TOK]

    def spread(code, values):
        total = jnp.zeros((TOK, TOK), F32)
        for k in range(TOP):
            value = 1.0 if values is None else values[k : k + 1]
            total = total + jnp.where(row_f == code[k : k + 1], value, 0.0)
        return total

    def top(p):
        return held.at[p, pl.ds(0, HALF)]

    def rest(p, rows):
        return held.at[p, pl.ds(HALF, rows)]

    routed, bare = HALF + META, HALF

    def onward(p):
        return at_z(lax.rem(z + jnp.where(lax.rem(p, 2) == 1, 1, NZ - 1), NZ))

    def take_top(p):
        arrived(top(p), r_z.at[p, 0])

        @pl.when(p < NZ - 2)
        def _():
            send(top(p), top(p + 2), s_z.at[0], r_z.at[p + 2, 0], onward(p))

    def take_rest(p):
        @pl.when(p < ZL)
        def _():
            arrived(rest(p, routed), r_z.at[p, 1])

        @pl.when(p >= ZL)
        def _():
            arrived(rest(p, bare), r_z.at[p, 1])

        @pl.when(p < ZL - 2)
        def _():
            send(rest(p, routed), rest(p + 2, routed), s_z.at[1], r_z.at[p + 2, 1], onward(p))

        @pl.when((p >= ZL - 2) & (p < NZ - 2))
        def _():
            send(rest(p, bare), rest(p + 2, bare), s_z.at[2], r_z.at[p + 2, 1], onward(p))

    def begin():
        for p, place in ((1, z + 1), (2, z + NZ - 1)):
            send(top(0), top(p), s_z.at[0], r_z.at[p, 0], at_z(lax.rem(place, NZ)))
        for p, place in ((1, z + 1), (2, z + NZ - 1)):
            send(rest(0, routed), rest(p, routed), s_z.at[1], r_z.at[p, 1], at_z(lax.rem(place, NZ)))

    def pack(p):
        block, half = source(p)
        code, weights = routing(p)
        pick = spread(code, None).astype(BF16)
        ysend[p] = dot(pick, held[p, 0:TOK, :]).astype(BF16)
        mine = block_rows(block, CAP, me * CAP)
        my_rows = pl.ds(pl.multiple_of(me * CAP, CAP), CAP)
        rows_x[0, half, mine, :] = ysend[p, my_rows, :]
        for d in FAR_FIRST:
            to = lax.rem(me + d, YC)
            theirs = pl.ds(pl.multiple_of(to * CAP, CAP), CAP)
            send(ysend.at[p, theirs, :], rows_x.at[0, half, mine, :], s_y, r_y.at[p], at_yc(to))

        @pl.when(p >= ZL)
        def _():
            q = p - ZL
            weight = jnp.sum(spread(code, weights), axis=1, keepdims=True)
            wsend[q] = jnp.broadcast_to(weight, (TOK, TOK)).astype(BF16)
            wrow[mine, :] = wsend[q, my_rows, :]
            for d in FAR_FIRST:
                to = lax.rem(me + d, YC)
                theirs = pl.ds(pl.multiple_of(to * CAP, CAP), CAP)
                send(wsend.at[q, theirs, :], wrow.at[mine, :], s_w, r_w.at[q], at_yc(to))

    def pass_on(p):
        block, half = source(p)
        arrived(ysend.at[p, pl.ds(0, TOK - CAP), :], r_y.at[p])

        @pl.when(p >= ZL)
        def _():
            arrived(wsend.at[p - ZL, pl.ds(0, TOK - CAP), :], r_w.at[p - ZL])

        low, high = block_rows(block, HALF), block_rows(block, HALF, HALF)
        send(rows_x.at[0, half, low, :], rows_x.at[1, half, low, :], s_x, r_x.at[p, 0], right)
        send(rows_x.at[0, half, high, :], rows_x.at[2, half, high, :], s_x, r_x.at[p, 1], left)
        send(rows_x.at[0, half, high, :], rows_x.at[1, half, high, :], s_x, r_x.at[p, 4], right)
        send(rows_x.at[0, half, low, :], rows_x.at[2, half, low, :], s_x, r_x.at[p, 5], left)

    def relay(p):
        block, half = source(p)
        low, high = block_rows(block, HALF), block_rows(block, HALF, HALF)
        arrived(rows_x.at[1, half, low, :], r_x.at[p, 0])
        send(rows_x.at[1, half, low, :], rows_x.at[3, half, low, :], s_x, r_x.at[p, 2], right)
        arrived(rows_x.at[2, half, high, :], r_x.at[p, 1])
        send(rows_x.at[2, half, high, :], rows_x.at[3, half, high, :], s_x, r_x.at[p, 3], left)

    def all_here(p):
        block, half = source(p)
        low, high = block_rows(block, HALF), block_rows(block, HALF, HALF)
        arrived(rows_x.at[1, half, high, :], r_x.at[p, 4])
        arrived(rows_x.at[2, half, low, :], r_x.at[p, 5])
        arrived(rows_x.at[3, half, low, :], r_x.at[p, 2])
        arrived(rows_x.at[3, half, high, :], r_x.at[p, 3])

    def features(slot, half):
        shift = (0, 3, 1, 2)[slot] if isinstance(slot, int) else jnp.where(
            slot == 0, 0, jnp.where(slot == 1, 3, slot - 1)
        )
        return pl.ds(pl.multiple_of((lax.rem(x + shift, NX) * ZH + half) * FS, FS), FS)

    def compute(p):
        q = p - ZL
        block, _ = source(p)
        rows = block_rows(block)
        a = jnp.zeros((TOK, HID), F32)
        u = jnp.zeros((TOK, HID), F32)
        g = jnp.zeros((TOK, HID), F32)
        for slot in range(NX):
            for half in range(ZH):
                f = features(slot, half)
                xs = rows_x[slot, half, rows, 0:FS]
                dys = rows_x[slot, half, rows, FS:WIDE]
                a = a + dot(xs, wg[:, f], 1, 1)
                u = u + dot(xs, wu[:, f], 1, 1)
                g = g + dot(dys, wd[:, f], 1, 1)
        weight = wrow[rows, :].astype(F32)[:, 0:1]
        sig = jax.nn.sigmoid(a)
        act = a * sig
        hidden = (act * u).astype(BF16).astype(F32)
        dp = jnp.sum((hidden * g).T, axis=0, keepdims=True)
        dpx[q, x] = jnp.broadcast_to(dp, (8, TOK))
        for d in range(1, NX):
            send(dpx.at[q, x], dpx.at[q, x], s_d, r_d.at[q], {"x": lax.rem(x + d, NX)})
        dh = weight * g
        d_a = dh * u * sig * (1.0 + a * (1.0 - sig))
        d_u = dh * act
        lanes = pl.ds(pl.multiple_of(block * TOK, TOK), TOK)
        dau_t[0:HID, lanes] = d_a.T.astype(BF16)
        dau_t[HID : 2 * HID, lanes] = d_u.T.astype(BF16)
        ph_t[:, lanes] = (weight * hidden).T.astype(BF16)
        d_a = d_a.astype(BF16)
        d_u = d_u.astype(BF16)
        for slot in (3, 2, 1, 0):
            for half in range(ZH):
                f = features(slot, half)
                to = slice(half * FS, half * FS + FS)
                term = dot(d_a, wg[:, f]) + dot(d_u, wu[:, f])
                if slot == 0:
                    own[q, :, to] = term
                elif slot == 3:
                    part_o[q, :, to] = term.astype(BF16)
                else:
                    part_rl[2 - slot, q, :, to] = term.astype(BF16)
            if slot == 3:
                send(part_o.at[q, pl.ds(0, HALF), :], buf_a.at[0, q], s_a, r_a.at[q, 0], right)
                send(part_o.at[q, pl.ds(HALF, HALF), :], buf_a.at[1, q], s_a, r_a.at[q, 1], left)

    def add_relay(p):
        q = p - ZL
        arrived(buf_a.at[0, q], r_a.at[q, 0])
        part_rl[0, q, 0:HALF, :] = (
            part_rl[0, q, 0:HALF, :].astype(F32) + buf_a[0, q].astype(F32)
        ).astype(BF16)
        send(part_rl.at[0, q], buf_b.at[0, q], s_b, r_b.at[q, 0], right)
        arrived(buf_a.at[1, q], r_a.at[q, 1])
        part_rl[1, q, HALF:TOK, :] = (
            part_rl[1, q, HALF:TOK, :].astype(F32) + buf_a[1, q].astype(F32)
        ).astype(BF16)
        send(part_rl.at[1, q], buf_b.at[1, q], s_b, r_b.at[q, 1], left)

    def send_back(p):
        q = p - ZL
        arrived(dpx.at[q, pl.ds(0, NX - 1)], r_d.at[q])
        dp = (dpx[q, 0] + dpx[q, 1]) + (dpx[q, 2] + dpx[q, 3])
        fsend[q, :, WIDE : WIDE + TOK] = jnp.broadcast_to(dp[0:1], (TOK, TOK)).T.astype(BF16)
        arrived(buf_b.at[0, q], r_b.at[q, 0])
        arrived(buf_b.at[1, q], r_b.at[q, 1])
        fsend[q, :, 0:WIDE] = (
            own[q] + buf_b[0, q].astype(F32) + buf_b[1, q].astype(F32)
        ).astype(BF16)
        my_rows = pl.ds(pl.multiple_of(me * CAP, CAP), CAP)
        frecv[q, my_rows, :] = fsend[q, my_rows, :]
        for d in FAR_FIRST:
            to = lax.rem(me + d, YC)
            theirs = pl.ds(pl.multiple_of(to * CAP, CAP), CAP)
            send(fsend.at[q, theirs, :], frecv.at[q, my_rows, :], s_f, r_f.at[q], at_yc(to))

    def combine(p, m):
        q = p - ZL
        block, far = source(p)
        near = 1 - far
        arrived(fsend.at[q, pl.ds(0, TOK - CAP), :], r_f.at[q])
        code, _ = routing(p)
        pick = spread(code, None).astype(BF16)
        dp = frecv[q, :, WIDE : WIDE + TOK].astype(F32)
        dp_rows = jnp.zeros((META, TOK), F32)
        for k in range(TOP):
            one = jnp.sum(jnp.where(row_f == code[k : k + 1], dp, 0.0), axis=0, keepdims=True)
            dp_rows = jnp.where(line == k, one, dp_rows)

        def gather(half):
            features_of = pl.ds(pl.multiple_of(half * FS, FS), FS)
            gsend[q, half, 0:TOK, :] = dot(pick, frecv[q, :, features_of], 0, 0).astype(BF16)
            gsend[q, half, TOK : TOK + META, 0:TOK] = dp_rows.astype(BF16)
            gsend[q, half, TOK : TOK + META, TOK : 2 * TOK] = jnp.zeros((META, TOK), BF16)

        gather(far)

        def place(to):
            away = lax.rem(to + NZ - z, NZ)
            return jnp.where(away < 5, away, away - 7)

        def add(half, n):
            arrived(chain.at[n], r_c.at[n])
            gsend[q, half] = (gsend[q, half].astype(F32) + chain[n].astype(F32)).astype(BF16)

        @pl.when((m >= 2) & (m < 7))
        def _():
            add(far, m)

        @pl.when(m < 7)
        def _():
            step = jnp.where(lax.rem(m, 2) == 0, 1, NZ - 1)
            send(gsend.at[q, far], chain.at[m + 2], s_c, r_c.at[m + 2], at_z(lax.rem(z + step, NZ)))

        @pl.when(m == 7)
        def _():
            add(far, 8)
            to = block + far * ZL
            send(gsend.at[q, far], zrecv.at[place(to)], s_g, r_g, at_z(to))

        gather(near)

        @pl.when(m == 7)
        def _():
            add(near, 7)

        @pl.when(m > 0)
        def _():
            to = block + near * ZL
            send(gsend.at[q, near], zrecv.at[place(to)], s_g, r_g, at_z(to))

        @pl.when(m == 0)
        def _():
            zrecv[0] = gsend[q, near]

    def weight_grads(slot):
        for half in range(ZH):
            f = features(slot, half)
            both = dot(dau_t[...], rows_x[slot, half, :, 0:FS])
            ggate[:, f] = both[0:HID].astype(BF16)
            gup[:, f] = both[HID : 2 * HID].astype(BF16)
            gdown[:, f] = dot(ph_t[...], rows_x[slot, half, :, FS:WIDE]).astype(BF16)

    def rank(j):
        m = j - ZL
        return jnp.where(m < 2, 1 - m, m)

    def turn(j):
        m = rank(j)
        late = jnp.where(lax.rem(j, 2) == 1, jnp.maximum(14 - m, ZL), jnp.minimum(NZ - m, NZ - 1))
        late = jnp.where(m == 0, NZ - 1, jnp.where(m == 1, NZ - 3, late))
        return jnp.where(j < ZL, j, late)

    def step(i, carry):
        def when(lag, least, act):
            j = i - lag

            @pl.when((j >= least) & (j < NZ))
            def _():
                act(turn(j), *((rank(j),) if act is combine else ()))

        def both(act):
            @pl.when((i > 0) & (i <= ZL))
            def _():
                act(2 * i - 1)

            @pl.when((i > 0) & (i < ZL))
            def _():
                act(2 * i)

        both(take_top)
        when(6, ZL, combine)
        when(1, 0, pass_on)
        both(take_rest)

        @pl.when(i < 2)
        def _():
            pack(turn(i))

        @pl.when((i > 0) & (i < NZ - 1))
        def _():
            pack(turn(i + 1))

        when(5, ZL, send_back)
        when(2, 0, relay)
        when(4, ZL, add_relay)
        when(3, 0, all_here)

        @pl.when(i == ZL)
        def _():
            for load in loads:
                load.wait()

        when(3, ZL, compute)

        @pl.when(i >= NZ + 2)
        def _():
            weight_grads(i - (NZ + 2))

        return carry

    begin()
    lax.fori_loop(0, NZ + 6, step, 0)
    for store in stores:
        store.start()

    arrived(zrecv.at[pl.ds(1, SUMS - 1)], r_g)
    total = jnp.zeros((TOK, FS), F32)
    dp = jnp.zeros((META, TOK), F32)
    for s in range(SUMS):
        total = total + zrecv[s, 0:TOK, :].astype(F32)
        dp = dp + zrecv[s, TOK : TOK + META, 0:TOK].astype(F32)
    gtok[...] = total.astype(BF16)
    gprob[...] = dp[0:TOP].astype(BF16)
    for store in stores:
        store.wait()

    arrived(held.at[pl.ds(0, NZ - 1), pl.ds(0, HALF)], s_z.at[0])
    arrived(held.at[pl.ds(0, ZL - 1), pl.ds(HALF, routed)], s_z.at[1])
    arrived(held.at[pl.ds(0, ZL), pl.ds(HALF, bare)], s_z.at[2])
    arrived(ysend.at[:, pl.ds(0, TOK - CAP), :], s_y)
    arrived(wsend.at[:, pl.ds(0, TOK - CAP), :], s_w)
    arrived(rows_x.at[pl.ds(1, NX - 1)], s_x)
    arrived(part_o, s_a)
    arrived(part_rl, s_b)
    arrived(fsend.at[:, pl.ds(0, TOK - CAP), :], s_f)
    arrived(zrecv.at[pl.ds(1, SUMS - 1)], s_g)
    arrived(chain.at[pl.ds(2, 7)], s_c)
    arrived(dpx.at[:, pl.ds(0, NX - 1)], s_d)


def hand_over(*refs):
    far, out, near, sems = refs[:5], refs[5:10], refs[10:15], refs[15]
    loads = [pltpu.make_async_copy(far[n], near[n], sems.at[0, n]) for n in range(5)]
    stores = [pltpu.make_async_copy(near[n], out[n], sems.at[1, n]) for n in range(5)]
    for load in loads:
        load.start()
    for load, store in zip(loads, stores):
        load.wait()
        store.start()
    for store in stores:
        store.wait()


def body(tokens, upstream, probs, expert_ids, gate_weight, up_weight, down_weight):
    vmem = pl.BlockSpec(memory_space=pltpu.VMEM)
    anywhere = pl.BlockSpec(memory_space=pl.ANY)
    dma = pltpu.SemaphoreType.DMA
    width = NX * ZH * FS
    out = (
        jax.ShapeDtypeStruct((TOK, FS), BF16),
        jax.ShapeDtypeStruct((TOP, TOK), BF16),
    ) + (jax.ShapeDtypeStruct((1, HID, width), BF16),) * 3
    results = pl.pallas_call(
        kernel,
        out_shape=out,
        in_specs=[vmem] * 4 + [anywhere] * 3,
        out_specs=(vmem,) * 2 + (anywhere,) * 3,
        scratch_shapes=[pltpu.VMEM((HID, width), BF16)] * 6
        + [
            dma((3,)), dma((3,)),
            pltpu.VMEM((NZ, TOK + META, WIDE), BF16),
            pltpu.VMEM((NZ, TOK, WIDE), BF16),
            pltpu.VMEM((ZL, TOK, TOK), BF16),
            pltpu.VMEM((NX, ZH, ZL * TOK, WIDE), BF16),
            pltpu.VMEM((ZL * TOK, TOK), BF16),
            pltpu.VMEM((2 * HID, ZL * TOK), BF16),
            pltpu.VMEM((HID, ZL * TOK), BF16),
            pltpu.VMEM((ZL, TOK, WIDE), F32),
            pltpu.VMEM((ZL, TOK, WIDE), BF16),
            pltpu.VMEM((2, ZL, TOK, WIDE), BF16),
            pltpu.VMEM((2, ZL, HALF, WIDE), BF16),
            pltpu.VMEM((2, ZL, TOK, WIDE), BF16),
            pltpu.VMEM((ZL, TOK, WIDE + TOK), BF16),
            pltpu.VMEM((ZL, TOK, WIDE + TOK), BF16),
            pltpu.VMEM((ZL, ZH, TOK + META, FS), BF16),
            pltpu.VMEM((SUMS, TOK + META, FS), BF16),
            pltpu.VMEM((9, TOK + META, FS), BF16),
            pltpu.VMEM((ZL, NX, 8, TOK), F32),
            dma((3,)), dma((NZ, 2)),
            dma, dma((NZ,)),
            dma, dma((ZL,)),
            dma, dma((NZ, 6)),
            dma, dma((ZL, 2)),
            dma, dma((ZL, 2)),
            dma, dma((ZL,)),
            dma, dma((9,)),
            dma, dma,
            dma, dma((ZL,)),
        ],
        compiler_params=pltpu.CompilerParams(
            collective_id=0, has_side_effects=True, vmem_limit_bytes=56 * 1024 * 1024
        ),
        cost_estimate=pl.CostEstimate(
            flops=16 * ZL * TOK * HID * width, bytes_accessed=8 << 20, transcendentals=0
        ),
    )(tokens, upstream, probs.T, expert_ids.T, gate_weight, up_weight, down_weight)
    tokens_out, probs_out, *weights_out = pl.pallas_call(
        hand_over,
        out_shape=out,
        in_specs=[anywhere] * 5,
        out_specs=(anywhere,) * 5,
        scratch_shapes=[pltpu.VMEM(o.shape, o.dtype) for o in out] + [dma((2, 5))],
    )(*results)
    return (tokens_out, probs_out.T, *weights_out)


def solution(mesh):
    parts = Mesh(mesh.devices.reshape(ZL, NY, NC, NX, ZH), ("zl", "y", "c", "x", "zh"))
    expert, tensor = ("zl", "y", "c"), ("x", "zh")
    placed = (
        P(expert, tensor),
        P(expert, tensor),
        P(expert, None),
        P(expert, None),
        P(expert, tensor, None),
        P(expert, tensor, None),
        P(expert, tensor, None),
    )
    return jax.shard_map(
        body,
        mesh=parts,
        in_specs=placed,
        out_specs=(
            P(expert, tensor),
            P(expert, None),
            P(expert, tensor, None),
            P(expert, tensor, None),
            P(expert, tensor, None),
        ),
        check_vma=False,
    )
```
